32 devices in a mesh: rep: 2 (over x), pool: 8 (over z, y), tp: 2 (over core).
Axes of the slice: x: 2, y: 2, z: 4, core: 2. Of those that a mesh axis runs over, the one named last changes fastest.
Arguments:
- hidden: bfloat16 [1024, 8192], P(('rep', 'pool')), parts along dimension 0, may hold values from -6 to 6
- base_query: bfloat16 [1024, 8192], P(('rep', 'pool'), 'tp'), parts along dimension 0, may hold values from -160 to 160
- key_cache: bfloat16 [1024, 64, 1024], P(('rep', 'pool'), None, 'tp'), parts along dimension 0, may hold values from -12 to 12
- value_cache: bfloat16 [1024, 64, 1024], P(('rep', 'pool'), None, 'tp'), parts along dimension 0, may hold values from -6 to 6
- new_key: bfloat16 [1024, 1024], P(('rep', 'pool'), 'tp'), parts along dimension 0, may hold values from -6 to 6
- new_value: bfloat16 [1024, 1024], P(('rep', 'pool'), 'tp'), parts along dimension 0, may hold values from -6 to 6
- lengths: int32 [1024], P(('rep', 'pool')), parts along dimension 0, may hold values from 2 to 64, as said below
- request_adapter: int32 [1024], P(('rep', 'pool')), parts along dimension 0, may hold values from 0 to 15, as said below
- adapter_store_row: int32 [32], P('rep'), parts along dimension 0, may hold values from 0 to 15, as said below
- adapter_down: bfloat16 [16, 8192, 64], P('pool', 'tp'), may hold values from -0.0625 to 0.0625
- adapter_up: bfloat16 [16, 64, 8192], P('pool', None, 'tp'), may hold values from -0.75 to 0.75
Outputs:
- context: bfloat16 [1024, 8192], P(('rep', 'pool'), 'tp'), parts along dimension 0
The draws below stay inside these ranges and needn't reach their ends.
There are 2 independent parts, one for each index of `rep`. The reference program is written for one: setup_inputs(seed, part) draws one part's arguments, and reference() takes and returns one part's arrays. A program takes and returns all parts, laid end to end along the dimension named above; an argument that names none is the same for every part. Nothing has to cross between parts.
Inputs may be any that keep to these rules, and one draw needn't show every extreme that they name: Each entry of each part is a different store row: a permutation. Adapter a lives with pool index adapter_store_row[a] // 2. `request_adapter`: within one group of 64 requests at most 16 requests have adapters held by one pool index; one pool index receives exactly 16 requests from every group. `lengths`: in every group some request uses all 64 positions.
All inputs are finite; a program needn't handle non-finite values.
Results may differ from the reference program's by a relative error of at most 0.0067.
Values may be sent and summed in bfloat16 or wider, within the bound.
No kernel may reach another device: no remote copies, remote signals or barrier semaphores. Data moves between devices by JAX's collectives and lax.ppermute only.
A program may use at most 64 MiB of HBM per device.

```python
import math
import jax
import jax.numpy as jnp
from jax import lax

MODEL_WIDTH = 8192
QUERY_HEADS = 64
KV_HEADS = 8
HEAD_SIZE = 128
ADAPTER_RANK = 64
REQ = 64
ADP_DEV = 2
LMAX = 64
REQUEST_TOTAL = 512
ADAPTER_TOTAL = 16
CAP = 16
QUERY_FEATURES = 8192
KVD = 1024


def storage_order(key):
    return jax.random.permutation(jax.random.fold_in(key, 101), ADAPTER_TOTAL).astype(jnp.int32)


def cache_noise(key):
    return jax.random.normal(jax.random.fold_in(key, 202), (REQUEST_TOTAL, LMAX, KV_HEADS * HEAD_SIZE), jnp.float32)


def draw_adapter_store_row(key, part):
    placed = storage_order(key)
    return placed


def draw_request_adapter(key, part):
    placed = storage_order(key)
    key = jax.random.fold_in(key, 2)
    adapter_at = jnp.argsort(placed, stable=True).astype(jnp.int32)
    owners = REQUEST_TOTAL // REQ
    slot_total = owners * CAP
    hot_key, row_key = jax.random.split(key, 2)
    favorite = jax.random.randint(hot_key, (), 0, owners)
    popular = jax.random.randint(jax.random.fold_in(hot_key, 1), (owners,), 0, 6) == 0
    owner_list = jnp.arange(owners, dtype=jnp.int32)
    extra_score = jnp.where(popular, 2048, 0) + jnp.where(owner_list == favorite, 4096, 0)
    slot_extra = jnp.repeat(extra_score, CAP)
    store_row_list = jnp.arange(slot_total, dtype=jnp.int32)

    def one_group(group_key):
        noise_key, order_key, local_key = jax.random.split(group_key, 3)
        noise = jax.random.randint(noise_key, (slot_total,), 0, 1024)
        ranking = (noise + slot_extra) * slot_total + store_row_list
        unused_value, chosen = lax.top_k(ranking, REQ)
        chosen = chosen[jax.random.permutation(order_key, REQ)]
        owner_pick = chosen // CAP
        local_pick = jax.random.randint(local_key, (REQ,), 0, ADP_DEV)
        return adapter_at[owner_pick * ADP_DEV + local_pick]
    drawn = jax.vmap(one_group)(jax.random.split(row_key, owners))
    return drawn.reshape(REQUEST_TOTAL).astype(jnp.int32)


def draw_lengths(key, part):
    key = jax.random.fold_in(key, 3)
    base_key, full_key = jax.random.split(key, 2)
    drawn = jax.random.randint(base_key, (REQUEST_TOTAL,), 2, LMAX + 1)
    full_row = jax.random.randint(full_key, (REQUEST_TOTAL // REQ,), 0, REQ)
    row_index = jnp.arange(REQUEST_TOTAL, dtype=jnp.int32)
    is_full = row_index % REQ == jnp.repeat(full_row, REQ)
    return jnp.where(is_full, LMAX, drawn).astype(jnp.int32)


def draw_key_cache(key, part):
    cached = cache_noise(key)
    return cached.astype(jnp.bfloat16)


def draw_base_query(key, part):
    key = jax.random.fold_in(key, 6)
    values = jax.random.normal(key, (REQUEST_TOTAL, QUERY_HEADS * HEAD_SIZE), jnp.float32)
    return values.astype(jnp.bfloat16)


def shard_levels(own_key, dims, cuts, low, high):
    level, own = 1.0, jax.random.fold_in(own_key, 6)
    for axis_at, shards_of in cuts:
        steps = jnp.exp(jax.random.uniform(jax.random.fold_in(own, axis_at), (shards_of,), jnp.float32, low / len(cuts), high / len(cuts)))
        level = level * jnp.repeat(steps, dims[axis_at] // shards_of).reshape([-1 if axis == axis_at else 1 for axis in range(len(dims))])
    return level


def bell_draw(rng, dims, scale, reach, shards=(), held_as=jnp.bfloat16):
    factor_of = shard_levels(rng, dims, shards, -0.22, 0.18) if shards else 1.0
    array = jax.random.normal(rng, dims, jnp.float32) * scale * factor_of
    return jnp.minimum(jnp.maximum(array, -reach), reach).astype(held_as)


def setup_inputs(seed: int = 0, part: int = 0) -> dict:
    key_of = jax.random.split(jax.random.key(seed), 12)
    part_splits = jax.random.split(jax.random.fold_in(key_of[11], part), 12)
    hidden = bell_draw(part_splits[0], (REQUEST_TOTAL, MODEL_WIDTH), 1.0, 6.0, ((0, 8),))
    base_query = draw_base_query(jax.random.fold_in(jax.random.fold_in(key_of[11], part), 71), part)
    key_cache = draw_key_cache(jax.random.fold_in(jax.random.fold_in(key_of[11], part), 71), part)
    value_cache = bell_draw(part_splits[3], (REQUEST_TOTAL, LMAX, KVD), 1.0, 6.0, ((0, 8), (2, 2)))
    new_key = bell_draw(part_splits[4], (REQUEST_TOTAL, KVD), 1.0, 6.0, ((0, 8), (1, 2)))
    new_value = bell_draw(part_splits[5], (REQUEST_TOTAL, KVD), 1.0, 6.0, ((0, 8), (1, 2)))
    lengths = draw_lengths(jax.random.fold_in(jax.random.fold_in(key_of[11], part), 71), part)
    request_adapter = draw_request_adapter(jax.random.fold_in(jax.random.fold_in(key_of[11], part), 71), part)
    adapter_store_row = draw_adapter_store_row(jax.random.fold_in(jax.random.fold_in(key_of[11], part), 71), part)
    adapter_down = bell_draw(key_of[9], (ADAPTER_TOTAL, MODEL_WIDTH, ADAPTER_RANK), MODEL_WIDTH ** -0.5, 0.0625, ((0, 8), (1, 2)))
    adapter_up = bell_draw(key_of[10], (ADAPTER_TOTAL, ADAPTER_RANK, QUERY_FEATURES), ADAPTER_RANK ** -0.5, 0.75, ((0, 8), (2, 2)))
    return {"hidden": hidden, "base_query": base_query, "key_cache": key_cache, "value_cache": value_cache, "new_key": new_key, "new_value": new_value, "lengths": lengths, "request_adapter": request_adapter, "adapter_store_row": adapter_store_row, "adapter_down": adapter_down, "adapter_up": adapter_up}


ADAPTER_SCALE = 2.0
MASKED = -1e+30

def attend_block(inputs):
    query_rows, cached_k, cached_v, fresh_k, fresh_v, limits = inputs
    count_rows = query_rows.shape[0]
    group_size = QUERY_HEADS // KV_HEADS
    heads_q = query_rows.reshape(count_rows, KV_HEADS, group_size, HEAD_SIZE)
    heads_k = cached_k.astype(jnp.float32).reshape(count_rows, LMAX, KV_HEADS, HEAD_SIZE)
    heads_v = cached_v.astype(jnp.float32).reshape(count_rows, LMAX, KV_HEADS, HEAD_SIZE)
    fresh_kh = fresh_k.astype(jnp.float32).reshape(count_rows, KV_HEADS, HEAD_SIZE)
    fresh_vh = fresh_v.astype(jnp.float32).reshape(count_rows, KV_HEADS, HEAD_SIZE)
    factor = 1.0 / math.sqrt(HEAD_SIZE)
    scores = jnp.einsum('rkgd,rpkd->rkgp', heads_q, heads_k) * factor
    usable = lax.broadcasted_iota(jnp.int32, (count_rows, LMAX), 1) < limits[:, None]
    scores = jnp.where(usable[:, None, None, :], scores, MASKED)
    own_score = jnp.einsum('rkgd,rkd->rkg', heads_q, fresh_kh) * factor
    highest = jnp.maximum(lax.optimization_barrier(jnp.max(scores, axis=-1)), own_score)
    weights = jnp.exp(scores - highest[..., None])
    own_weight = jnp.exp(own_score - highest)
    totals = lax.optimization_barrier(jnp.sum(weights, axis=-1)) + own_weight
    weights_b = lax.optimization_barrier(weights.astype(jnp.bfloat16))
    own_b = lax.optimization_barrier(own_weight.astype(jnp.bfloat16))
    mixed = jnp.einsum('rkgp,rpkd->rkgd', weights_b.astype(jnp.float32), heads_v)
    mixed = mixed + own_b.astype(jnp.float32)[..., None] * fresh_vh[:, :, None, :]
    mixed = mixed / totals[..., None]
    return mixed.reshape(count_rows, QUERY_HEADS * HEAD_SIZE).astype(jnp.bfloat16)

def reference(hidden, base_query, key_cache, value_cache, new_key, new_value, lengths, request_adapter, adapter_store_row, adapter_down, adapter_up):
    position = adapter_store_row[request_adapter].astype(jnp.int32)
    store_row_list = jnp.arange(ADAPTER_TOTAL, dtype=jnp.int32)

    def down_project(carried, store_row_number):
        matrix_product = jnp.dot(hidden, adapter_down[store_row_number], preferred_element_type=jnp.float32)
        return (carried + jnp.where((position == store_row_number)[:, None], matrix_product, 0.0), None)
    adapter_middle, unused_value = lax.scan(down_project, jnp.zeros((REQUEST_TOTAL, ADAPTER_RANK), jnp.float32), store_row_list)
    middle_batch = adapter_middle.astype(jnp.bfloat16)

    def up_project(carried, store_row_number):
        matrix_product = jnp.dot(middle_batch, adapter_up[store_row_number], preferred_element_type=jnp.float32)
        return (carried + jnp.where((position == store_row_number)[:, None], matrix_product, 0.0), None)
    adapter_output, unused_value = lax.scan(up_project, jnp.zeros((REQUEST_TOTAL, QUERY_HEADS * HEAD_SIZE), jnp.float32), store_row_list)
    adapter_delta = lax.optimization_barrier((ADAPTER_SCALE * adapter_output).astype(jnp.bfloat16))
    query_rows = base_query.astype(jnp.float32) + adapter_delta.astype(jnp.float32)
    blocks = REQUEST_TOTAL // REQ
    pieces = (query_rows.reshape(blocks, REQ, QUERY_HEADS * HEAD_SIZE), key_cache.reshape(blocks, REQ, LMAX, KV_HEADS * HEAD_SIZE), value_cache.reshape(blocks, REQ, LMAX, KV_HEADS * HEAD_SIZE), new_key.reshape(blocks, REQ, KV_HEADS * HEAD_SIZE), new_value.reshape(blocks, REQ, KV_HEADS * HEAD_SIZE), lengths.reshape(blocks, REQ))
    context = lax.map(attend_block, pieces)
    return context.reshape(REQUEST_TOTAL, QUERY_HEADS * HEAD_SIZE)
```

```python
import functools
import math

import jax
import jax.numpy as jnp
from jax import lax
from jax.experimental import pallas as pl
from jax.experimental.pallas import tpu as pltpu
from jax.sharding import PartitionSpec as P

HEAD_SIZE = 128
ADAPTER_SCALE = 2.0
MASKED = -1e30
LANES = 128
ROWS = 16
MIB = 1024 * 1024

VMEM = pl.BlockSpec(memory_space=pltpu.VMEM)
ANYWHERE = pl.BlockSpec(memory_space=pl.ANY)


def grant(mib):
    return pltpu.CompilerParams(vmem_limit_bytes=mib * MIB)


def column_of(row):
    count = row.shape[1]
    here = lax.broadcasted_iota(jnp.int32, (count, count), 0)
    there = lax.broadcasted_iota(jnp.int32, (count, count), 1)
    spread = jnp.broadcast_to(row, (count, count))
    return jnp.sum(jnp.where(here == there, spread, 0), axis=1, keepdims=True)


def as_bf16(mask):
    return mask.astype(jnp.float32).astype(jnp.bfloat16)


def pack_kernel(pool_count, capacity, owned_count, splits, adapter_hbm, store_hbm, hidden_hbm, *refs):
    outs = refs[: len(splits)]
    routing_ref, adapter_ref, store_ref, held_ref, sems, index_sems = refs[len(splits) :]
    width = held_ref.shape[1]
    chunks = sems.shape[0]
    step = width // chunks
    start = lax.axis_index("tp") * width
    small = [
        pltpu.make_async_copy(adapter_hbm, adapter_ref, index_sems.at[0]),
        pltpu.make_async_copy(store_hbm, store_ref, index_sems.at[1]),
    ]
    copies = [
        pltpu.make_async_copy(
            hidden_hbm.at[:, pl.ds(pl.multiple_of(start + c * step, LANES), step)],
            held_ref.at[:, pl.ds(c * step, step)],
            sems.at[c],
        )
        for c in range(chunks)
    ]
    for copy in small + copies:
        copy.start()
    for copy in small:
        copy.wait()
    adapters = store_ref.shape[1]
    requests = adapter_ref.shape[1]
    matches = lax.broadcasted_iota(jnp.int32, (adapters, requests), 0) == adapter_ref[...]
    position = jnp.sum(jnp.where(matches, column_of(store_ref[...]), 0), axis=0, keepdims=True)
    owner = lax.div(position, jnp.int32(owned_count))
    held = position - owner * owned_count
    distance = lax.bitwise_xor(owner, jnp.broadcast_to(lax.axis_index("pool"), owner.shape))
    earlier = lax.broadcasted_iota(jnp.int32, (requests, requests), 0) < lax.broadcasted_iota(
        jnp.int32, (requests, requests), 1
    )
    same = column_of(owner) == owner
    rank = jnp.sum(jnp.where(same & earlier, 1, 0), axis=0, keepdims=True)
    target = distance * capacity + rank
    slot_total = pool_count * capacity
    routing = lax.broadcasted_iota(jnp.int32, (slot_total, requests), 0) == target
    held_slot = jnp.sum(jnp.where(routing, held, 0), axis=1, keepdims=True)
    tags = jnp.broadcast_to(held_slot, (slot_total, LANES)).astype(jnp.float32).astype(jnp.bfloat16)
    routing_b = as_bf16(routing)
    back = lax.broadcasted_iota(jnp.int32, (requests, slot_total), 1) == column_of(target)
    routing_ref[...] = as_bf16(back)
    for out, (first, size) in zip(outs, splits):
        out[:, width:] = tags[first : first + size]
    for c, copy in enumerate(copies):
        copy.wait()
        columns = slice(c * step, (c + 1) * step)
        packed = jnp.dot(
            routing_b, held_ref[:, columns], preferred_element_type=jnp.float32
        ).astype(jnp.bfloat16)
        for out, (first, size) in zip(outs, splits):
            out[:, columns] = packed[first : first + size]


def pack(hidden, request_adapter, adapter_store_row, pool_count, capacity, owned_count, width, splits):
    requests = hidden.shape[0]
    adapters = adapter_store_row.shape[0]
    slot_total = pool_count * capacity
    chunks = 4
    return pl.pallas_call(
        functools.partial(pack_kernel, pool_count, capacity, owned_count, splits),
        out_shape=[jax.ShapeDtypeStruct((size, width + LANES), jnp.bfloat16) for _, size in splits]
        + [jax.ShapeDtypeStruct((requests, slot_total), jnp.bfloat16)],
        in_specs=[ANYWHERE] * 3,
        out_specs=[VMEM] * (len(splits) + 1),
        scratch_shapes=[
            pltpu.VMEM((1, requests), jnp.int32),
            pltpu.VMEM((1, adapters), jnp.int32),
            pltpu.VMEM((requests, width), jnp.bfloat16),
            pltpu.SemaphoreType.DMA((chunks,)),
            pltpu.SemaphoreType.DMA((2,)),
        ],
        compiler_params=grant(8),
        name="pack",
    )(request_adapter.reshape(1, requests), adapter_store_row.reshape(1, adapters), hidden)


def down_kernel(count, *refs):
    rows, down_ref, out_ref = refs[:count], refs[count], refs[count + 1]
    owned_count, _, width = down_ref.shape
    features = jnp.concatenate([row[:, :width] for row in rows], axis=0)
    tags = jnp.concatenate([row[:, width : width + 1] for row in rows], axis=0).astype(jnp.float32)
    total = jnp.zeros(out_ref.shape, jnp.float32)
    for slot in range(owned_count):
        partial = lax.dot_general(
            features,
            down_ref[slot],
            (((1,), (1,)), ((), ())),
            preferred_element_type=jnp.float32,
        )
        total = total + jnp.where(tags == float(slot), partial, 0.0)
    out_ref[...] = total


def down(rows, adapter_down):
    total = sum(row.shape[0] for row in rows)
    rank = adapter_down.shape[1]
    return pl.pallas_call(
        functools.partial(down_kernel, len(rows)),
        out_shape=jax.ShapeDtypeStruct((total, rank), jnp.float32),
        in_specs=[VMEM] * (len(rows) + 1),
        out_specs=VMEM,
        compiler_params=grant(8),
        cost_estimate=pl.CostEstimate(
            flops=2 * total * adapter_down.size, bytes_accessed=2 * adapter_down.size, transcendentals=0
        ),
        name="down",
    )(*rows, adapter_down)


def up_kernel(count, mine_ref, other_ref, up_ref, *refs):
    rows, outs = refs[:count], refs[count:]
    owned_count, _, width = up_ref.shape
    tags = jnp.concatenate([row[:, :1] for row in rows], axis=0).astype(jnp.float32)
    middle = (mine_ref[...] + other_ref[...]).astype(jnp.bfloat16).astype(jnp.float32)
    chosen = jnp.concatenate(
        [jnp.where(tags == float(slot), middle, 0.0) for slot in range(owned_count)], axis=1
    ).astype(jnp.bfloat16)
    step = min(width, 1024)
    for c in range(width // step):
        columns = slice(c * step, (c + 1) * step)
        factors = jnp.concatenate([up_ref[slot, :, columns] for slot in range(owned_count)], axis=0)
        total = jnp.dot(chosen, factors, preferred_element_type=jnp.float32)
        total = (ADAPTER_SCALE * total).astype(jnp.bfloat16)
        at = 0
        for out in outs:
            out[:, columns] = total[at : at + out.shape[0]]
            at += out.shape[0]


def up(mine, other, rows, adapter_up):
    width = adapter_up.shape[2]
    total = mine.shape[0]
    tag_at = rows[0].shape[1] // LANES - 1
    return pl.pallas_call(
        functools.partial(up_kernel, len(rows)),
        grid=(1,),
        out_shape=[jax.ShapeDtypeStruct((row.shape[0], width), jnp.bfloat16) for row in rows],
        in_specs=[VMEM] * 3
        + [pl.BlockSpec((row.shape[0], LANES), lambda i: (0, tag_at)) for row in rows],
        out_specs=[VMEM] * len(rows),
        compiler_params=grant(8),
        cost_estimate=pl.CostEstimate(
            flops=2 * total * adapter_up.size, bytes_accessed=2 * adapter_up.size, transcendentals=0
        ),
        name="up",
    )(mine, other, adapter_up, *rows)


def serve(rows, adapter_down, adapter_up, tp_count):
    mine = down(rows, adapter_down)
    other = lax.ppermute(mine, "tp", [(i, tp_count - 1 - i) for i in range(tp_count)])
    return up(mine, other, rows, adapter_up)


def prepare_kernel(base_ref, lengths_ref, heads_ref, valid_ref):
    requests = base_ref.shape[0]
    cached_count, rows, _ = heads_ref.shape
    group_size = rows // requests
    for j in range(cached_count):
        for h in range(group_size):
            at = (j * group_size + h) * HEAD_SIZE
            heads_ref[j, pl.ds(h, requests, stride=group_size), :] = base_ref[
                :, at : at + HEAD_SIZE
            ].astype(jnp.float32)
    cached_len = valid_ref.shape[1] - requests
    place = lax.broadcasted_iota(jnp.int32, (requests, cached_len + requests), 1)
    own = place - cached_len == lax.broadcasted_iota(jnp.int32, place.shape, 0)
    inside = (place < column_of(lengths_ref[...])) & (place < cached_len)
    allowed = (inside | own).astype(jnp.float32)
    for h in range(group_size):
        valid_ref[pl.ds(h, requests, stride=group_size), :] = allowed


def prepare(base_query, lengths, cached_len, cached_count):
    requests, features = base_query.shape
    rows = requests * features // (HEAD_SIZE * cached_count)
    return pl.pallas_call(
        prepare_kernel,
        out_shape=[
            jax.ShapeDtypeStruct((cached_count, rows, HEAD_SIZE), jnp.float32),
            jax.ShapeDtypeStruct((rows, cached_len + requests), jnp.float32),
        ],
        in_specs=[VMEM] * 2,
        out_specs=[VMEM] * 2,
        compiler_params=grant(8),
        name="prepare",
    )(base_query, lengths.reshape(1, requests))


def attend_kernel(
    count, heads_ref, valid_ref, routing_ref, key_ref, value_ref, fresh_k_ref, fresh_v_ref, *refs
):
    returned, out_ref, delta_ref, score_ref, mixed_ref = refs[:count], *refs[count:]
    requests, cached_len, _ = key_ref.shape
    cached_count, rows, _ = heads_ref.shape
    group_size = rows // requests
    factor = 1.0 / math.sqrt(HEAD_SIZE)
    across = (((1,), (1,)), ((), ()))
    for j in range(cached_count):
        lanes = slice(j * HEAD_SIZE, (j + 1) * HEAD_SIZE)
        wide = slice(j * group_size * HEAD_SIZE, (j + 1) * group_size * HEAD_SIZE)
        arrived = jnp.concatenate([piece[:, wide] for piece in returned], axis=0)
        delta = jnp.dot(routing_ref[...], arrived, preferred_element_type=jnp.float32)
        for h in range(group_size):
            delta_ref[pl.ds(h, requests, stride=group_size), :] = delta[
                :, h * HEAD_SIZE : (h + 1) * HEAD_SIZE
            ]
        for r in range(requests):
            here = slice(r * group_size, (r + 1) * group_size)
            pair = jnp.concatenate([heads_ref[j, here, :], delta_ref[here, :]], axis=0)
            both = lax.dot_general(
                pair.astype(jnp.bfloat16),
                key_ref[r, :, lanes],
                across,
                preferred_element_type=jnp.float32,
            )
            score_ref[here, :cached_len] = both[:group_size] + both[group_size:]
        own = lax.dot_general(
            heads_ref[j].astype(jnp.bfloat16),
            fresh_k_ref[:, lanes],
            across,
            preferred_element_type=jnp.float32,
        ) + lax.dot_general(
            delta_ref[...].astype(jnp.bfloat16),
            fresh_k_ref[:, lanes],
            across,
            preferred_element_type=jnp.float32,
        )
        score_ref[:, cached_len:] = own
        scores = jnp.where(valid_ref[...] > 0.0, score_ref[...] * factor, MASKED)
        highest = jnp.max(scores, axis=1, keepdims=True)
        weights = jnp.exp(scores - highest)
        totals = jnp.sum(weights, axis=1, keepdims=True)
        weights_b = weights.astype(jnp.bfloat16)
        score_ref[...] = weights_b.astype(jnp.float32)
        own_mixed = jnp.dot(
            weights_b[:, cached_len:], fresh_v_ref[:, lanes], preferred_element_type=jnp.float32
        )
        for r in range(requests):
            here = slice(r * group_size, (r + 1) * group_size)
            mixed_ref[here, :] = jnp.dot(
                score_ref[here, :cached_len].astype(jnp.bfloat16),
                value_ref[r, :, lanes],
                preferred_element_type=jnp.float32,
            )
        mixed_ref[...] = (mixed_ref[...] + own_mixed) / totals
        for h in range(group_size):
            at = (j * group_size + h) * HEAD_SIZE
            out_ref[:, at : at + HEAD_SIZE] = mixed_ref[
                pl.ds(h, requests, stride=group_size), :
            ].astype(jnp.bfloat16)


def attend(heads, valid, routing_b, key_cache, value_cache, new_key, new_value, returned):
    requests, cached_len, _ = key_cache.shape
    cached_count, rows, _ = heads.shape
    features = cached_count * rows // requests * HEAD_SIZE
    return pl.pallas_call(
        functools.partial(attend_kernel, len(returned)),
        out_shape=jax.ShapeDtypeStruct((requests, features), jnp.bfloat16),
        in_specs=[VMEM] * (7 + len(returned)),
        out_specs=VMEM,
        scratch_shapes=[
            pltpu.VMEM((rows, HEAD_SIZE), jnp.float32),
            pltpu.VMEM((rows, cached_len + requests), jnp.float32),
            pltpu.VMEM((rows, HEAD_SIZE), jnp.float32),
        ],
        compiler_params=grant(20),
        name="attend",
    )(heads, valid, routing_b, key_cache, value_cache, new_key, new_value, *returned)


def after(arrays, *tokens):
    return lax.optimization_barrier((tuple(arrays), tokens))[0]


def shards(
    hidden,
    base_query,
    key_cache,
    value_cache,
    new_key,
    new_value,
    lengths,
    request_adapter,
    adapter_store_row,
    adapter_down,
    adapter_up,
):
    request_rows = hidden.shape[0]
    pool_count = lax.axis_size("pool")
    tp_count = lax.axis_size("tp")
    capacity = max(2, 2 * request_rows // pool_count)
    slot_total = pool_count * capacity
    owned_count, half_width, _ = adapter_down.shape
    cached_len = key_cache.shape[1]
    cached_count = key_cache.shape[2] // HEAD_SIZE
    per_group = max(1, ROWS // capacity)
    group_rows = per_group * capacity
    group_count = slot_total // group_rows
    splits = [(g * group_rows, group_rows) for g in range(group_count)]
    adapter_down = jnp.swapaxes(adapter_down, 1, 2)

    def travel(g, rows):
        parts = []
        for k in range(per_group):
            distance = g * per_group + k
            part = rows[k * capacity : (k + 1) * capacity] if per_group > 1 else rows
            if distance:
                part = lax.ppermute(part, "pool", [(i, i ^ distance) for i in range(pool_count)])
            parts.append(part)
        return parts[0] if per_group == 1 else jnp.concatenate(parts, axis=0)

    near = list(range(group_count // 2))
    far = list(range(group_count // 2, group_count))
    first, second = far[: len(far) // 2], far[len(far) // 2 :]
    *groups, routing_b = pack(
        hidden, request_adapter, adapter_store_row, pool_count, capacity, owned_count, half_width, splits
    )
    heads, valid = prepare(base_query, lengths, cached_len, cached_count)
    arrived = {g: travel(g, groups[g]) for g in first + near}
    late = after([groups[g] for g in second], arrived[near[1]])
    arrived |= {g: travel(g, rows) for g, rows in zip(second, late)}
    returned = {}
    for chosen in (first + near, second):
        served = serve([arrived[g] for g in chosen], adapter_down, adapter_up, tp_count)
        returned |= {g: travel(g, rows) for g, rows in zip(chosen, served)}
    return attend(
        heads,
        valid,
        routing_b,
        key_cache,
        value_cache,
        new_key,
        new_value,
        [returned[g] for g in range(group_count)],
    )


def solution(mesh):
    placed = (
        P(("rep", "pool"), None),
        P(("rep", "pool"), "tp"),
        P(("rep", "pool"), None, "tp"),
        P(("rep", "pool"), None, "tp"),
        P(("rep", "pool"), "tp"),
        P(("rep", "pool"), "tp"),
        P(("rep", "pool")),
        P(("rep", "pool")),
        P("rep"),
        P("pool", "tp", None),
        P("pool", None, "tp"),
    )
    return jax.shard_map(
        shards, mesh=mesh, in_specs=placed, out_specs=P(("rep", "pool"), "tp"), check_vma=False
    )
```

```python
import functools
import math

import jax
import jax.numpy as jnp
from jax import lax
from jax.experimental import pallas as pl
from jax.experimental.pallas import tpu as pltpu
from jax.sharding import PartitionSpec as P

HEAD_SIZE = 128
ADAPTER_SCALE = 2.0
MASKED = -1e30
LANES = 128
ROWS = 16
MIB = 1024 * 1024

VMEM = pl.BlockSpec(memory_space=pltpu.VMEM)
ANYWHERE = pl.BlockSpec(memory_space=pl.ANY)


def grant(mib):
    return pltpu.CompilerParams(vmem_limit_bytes=mib * MIB)


def column_of(row):
    count = row.shape[1]
    here = lax.broadcasted_iota(jnp.int32, (count, count), 0)
    there = lax.broadcasted_iota(jnp.int32, (count, count), 1)
    spread = jnp.broadcast_to(row, (count, count))
    return jnp.sum(jnp.where(here == there, spread, 0), axis=1, keepdims=True)


def in_hbm(array):
    return pltpu.with_memory_space_constraint(array, pltpu.HBM)


def as_bf16(mask):
    return mask.astype(jnp.float32).astype(jnp.bfloat16)


def pack_kernel(pool_count, tp_count, capacity, owned_count, adapter_hbm, store_hbm, hidden_hbm, *refs):
    *outs, routing_ref, adapter_ref, store_ref, held_ref, sems, index_sems = refs
    width = held_ref.shape[1]
    chunks = sems.shape[0]
    step = width // chunks
    small = [
        pltpu.make_async_copy(adapter_hbm, adapter_ref, index_sems.at[0]),
        pltpu.make_async_copy(store_hbm, store_ref, index_sems.at[1]),
    ]
    copies = [
        pltpu.make_async_copy(
            hidden_hbm.at[:, pl.ds(c * step, step)], held_ref.at[:, pl.ds(c * step, step)], sems.at[c]
        )
        for c in range(chunks)
    ]
    for copy in small + copies:
        copy.start()
    for copy in small:
        copy.wait()
    adapters = store_ref.shape[1]
    requests = adapter_ref.shape[1]
    slot_total = pool_count // tp_count * capacity
    matches = lax.broadcasted_iota(jnp.int32, (adapters, requests), 0) == adapter_ref[...]
    position = jnp.sum(jnp.where(matches, column_of(store_ref[...]), 0), axis=0, keepdims=True)
    owner = lax.div(position, jnp.int32(owned_count))
    held = position - owner * owned_count
    distance = lax.bitwise_xor(owner, jnp.broadcast_to(lax.axis_index("pool"), owner.shape))
    step_of = lax.div(distance, jnp.int32(tp_count))
    mine = distance - step_of * tp_count == lax.axis_index("tp")
    earlier = lax.broadcasted_iota(jnp.int32, (requests, requests), 0) < lax.broadcasted_iota(
        jnp.int32, (requests, requests), 1
    )
    same = column_of(owner) == owner
    rank = jnp.sum(jnp.where(same & earlier, 1, 0), axis=0, keepdims=True)
    target = step_of * capacity + rank + jnp.where(mine, 0, slot_total)
    routing = lax.broadcasted_iota(jnp.int32, (slot_total, requests), 0) == target
    held_slot = jnp.sum(jnp.where(routing, held, 0), axis=1, keepdims=True)
    tags = jnp.broadcast_to(held_slot, (slot_total, LANES)).astype(jnp.float32).astype(jnp.bfloat16)
    routing_b = as_bf16(routing)
    back = lax.broadcasted_iota(jnp.int32, (requests, tp_count * slot_total), 1) == column_of(target)
    routing_ref[...] = as_bf16(back)
    for g, out in enumerate(outs):
        out[:, width:] = tags[g * out.shape[0] : (g + 1) * out.shape[0]]
    for c, copy in enumerate(copies):
        copy.wait()
        columns = slice(c * step, (c + 1) * step)
        packed = jnp.dot(
            routing_b, held_ref[:, columns], preferred_element_type=jnp.float32
        ).astype(jnp.bfloat16)
        for g, out in enumerate(outs):
            out[:, columns] = packed[g * out.shape[0] : (g + 1) * out.shape[0]]


def pack(hidden, request_adapter, adapter_store_row, pool_count, tp_count, capacity, owned_count, group_rows):
    requests, width = hidden.shape
    adapters = adapter_store_row.shape[0]
    slot_total = pool_count // tp_count * capacity
    group_count = slot_total // group_rows
    chunks = 4
    return pl.pallas_call(
        functools.partial(pack_kernel, pool_count, tp_count, capacity, owned_count),
        out_shape=[pltpu.VMEM((group_rows, width + LANES), jnp.bfloat16)] * group_count
        + [pltpu.VMEM((requests, tp_count * slot_total), jnp.bfloat16)],
        in_specs=[ANYWHERE] * 3,
        out_specs=[VMEM] * (group_count + 1),
        scratch_shapes=[
            pltpu.VMEM((1, requests), jnp.int32),
            pltpu.VMEM((1, adapters), jnp.int32),
            pltpu.VMEM((requests, width), jnp.bfloat16),
            pltpu.SemaphoreType.DMA((chunks,)),
            pltpu.SemaphoreType.DMA((2,)),
        ],
        compiler_params=grant(8),
        name="pack",
    )(
        in_hbm(request_adapter.reshape(1, requests)),
        in_hbm(adapter_store_row.reshape(1, adapters)),
        in_hbm(hidden),
    )


def serve_kernel(count, *refs):
    rows, (down_ref, down_far_ref, up_ref, up_far_ref), outs = (
        refs[:count],
        refs[count : count + 4],
        refs[count + 4 :],
    )
    owned_count, rank, width = down_ref.shape
    here = lax.axis_index("tp")
    there = 1 - here
    tags = jnp.concatenate([row[:, 2 * width : 2 * width + 1] for row in rows], axis=0)
    tags = tags.astype(jnp.float32)
    middle = jnp.zeros((tags.shape[0], rank), jnp.float32)
    for half, factors in ((here, down_ref), (there, down_far_ref)):
        columns = pl.ds(pl.multiple_of(half * width, LANES), width)
        features = jnp.concatenate([row[:, columns] for row in rows], axis=0)
        for slot in range(owned_count):
            partial = lax.dot_general(
                features,
                factors[slot],
                (((1,), (1,)), ((), ())),
                preferred_element_type=jnp.float32,
            )
            middle = middle + jnp.where(tags == float(slot), partial, 0.0)
    middle = middle.astype(jnp.bfloat16).astype(jnp.float32)
    chosen = jnp.concatenate(
        [jnp.where(tags == float(slot), middle, 0.0) for slot in range(owned_count)], axis=1
    ).astype(jnp.bfloat16)
    step = min(width, 1024)
    for half, factors in ((here, up_ref), (there, up_far_ref)):
        for c in range(width // step):
            columns = slice(c * step, (c + 1) * step)
            stacked = jnp.concatenate([factors[slot, :, columns] for slot in range(owned_count)], axis=0)
            total = jnp.dot(chosen, stacked, preferred_element_type=jnp.float32)
            total = (ADAPTER_SCALE * total).astype(jnp.bfloat16)
            at = 0
            for out in outs:
                out[half, :, columns] = total[at : at + out.shape[1]]
                at += out.shape[1]


def serve(rows, factors):
    width = factors[0].shape[2]
    return pl.pallas_call(
        functools.partial(serve_kernel, len(rows)),
        out_shape=[pltpu.VMEM((2, row.shape[0], width), jnp.bfloat16) for row in rows],
        in_specs=[VMEM] * (len(rows) + 4),
        out_specs=[VMEM] * len(rows),
        compiler_params=grant(8),
        name="serve",
    )(*rows, *factors)


def prepare_kernel(
    base_hbm,
    lengths_hbm,
    down_hbm,
    up_hbm,
    key_hbm,
    value_hbm,
    heads_ref,
    valid_ref,
    down_ref,
    up_ref,
    key_ref,
    value_ref,
    base_ref,
    lengths_ref,
    sems,
):
    pairs = [
        (lengths_hbm, lengths_ref),
        (base_hbm, base_ref),
        (down_hbm, down_ref),
        (up_hbm, up_ref),
        (key_hbm, key_ref),
        (value_hbm, value_ref),
    ]
    copies = [pltpu.make_async_copy(*pair, sems.at[i]) for i, pair in enumerate(pairs)]
    for copy in copies:
        copy.start()
    copies[0].wait()
    copies[1].wait()
    requests = base_ref.shape[0]
    cached_count, rows, _ = heads_ref.shape
    group_size = rows // requests
    for j in range(cached_count):
        for h in range(group_size):
            at = (j * group_size + h) * HEAD_SIZE
            heads_ref[j, pl.ds(h, requests, stride=group_size), :] = base_ref[
                :, at : at + HEAD_SIZE
            ].astype(jnp.float32)
    cached_len = valid_ref.shape[1] - requests
    place = lax.broadcasted_iota(jnp.int32, (requests, cached_len + requests), 1)
    own = place - cached_len == lax.broadcasted_iota(jnp.int32, place.shape, 0)
    inside = (place < column_of(lengths_ref[...])) & (place < cached_len)
    allowed = (inside | own).astype(jnp.float32)
    for h in range(group_size):
        valid_ref[pl.ds(h, requests, stride=group_size), :] = allowed
    for copy in copies[2:]:
        copy.wait()


def prepare(base_query, lengths, adapter_down, adapter_up, key_cache, value_cache):
    requests, features = base_query.shape
    cached_len = key_cache.shape[1]
    cached_count = key_cache.shape[2] // HEAD_SIZE
    rows = requests * features // (HEAD_SIZE * cached_count)
    held = [adapter_down, adapter_up, key_cache, value_cache]
    return pl.pallas_call(
        prepare_kernel,
        out_shape=[
            pltpu.VMEM((cached_count, rows, HEAD_SIZE), jnp.float32),
            pltpu.VMEM((rows, cached_len + requests), jnp.float32),
        ]
        + [pltpu.VMEM(array.shape, array.dtype) for array in held],
        in_specs=[ANYWHERE] * 6,
        out_specs=[VMEM] * 6,
        scratch_shapes=[
            pltpu.VMEM((requests, features), base_query.dtype),
            pltpu.VMEM((1, requests), jnp.int32),
            pltpu.SemaphoreType.DMA((6,)),
        ],
        compiler_params=grant(8),
        cost_estimate=pl.CostEstimate(
            flops=0, bytes_accessed=4 * key_cache.size + 4 * adapter_up.size, transcendentals=0
        ),
        name="prepare",
    )(*[in_hbm(array) for array in [base_query, lengths.reshape(1, requests)] + held])


def attend_kernel(
    count, heads_ref, valid_ref, routing_ref, key_ref, value_ref, fresh_k_ref, fresh_v_ref, *refs
):
    returned, out_ref, delta_ref, score_ref, mixed_ref = refs[:count], *refs[count:]
    requests, cached_len, _ = key_ref.shape
    cached_count, rows, _ = heads_ref.shape
    group_size = rows // requests
    factor = 1.0 / math.sqrt(HEAD_SIZE)
    across = (((1,), (1,)), ((), ()))
    half = lax.axis_index("tp")
    for j in range(cached_count):
        lanes = slice(j * HEAD_SIZE, (j + 1) * HEAD_SIZE)
        wide = slice(j * group_size * HEAD_SIZE, (j + 1) * group_size * HEAD_SIZE)
        arrived = jnp.concatenate([piece[half, :, wide] for piece in returned], axis=0)
        delta = jnp.dot(routing_ref[...], arrived, preferred_element_type=jnp.float32)
        for h in range(group_size):
            delta_ref[pl.ds(h, requests, stride=group_size), :] = delta[
                :, h * HEAD_SIZE : (h + 1) * HEAD_SIZE
            ]
        for r in range(requests):
            here = slice(r * group_size, (r + 1) * group_size)
            pair = jnp.concatenate([heads_ref[j, here, :], delta_ref[here, :]], axis=0)
            both = lax.dot_general(
                pair.astype(jnp.bfloat16),
                key_ref[r, :, lanes],
                across,
                preferred_element_type=jnp.float32,
            )
            score_ref[here, :cached_len] = both[:group_size] + both[group_size:]
        own = lax.dot_general(
            heads_ref[j].astype(jnp.bfloat16),
            fresh_k_ref[:, lanes],
            across,
            preferred_element_type=jnp.float32,
        ) + lax.dot_general(
            delta_ref[...].astype(jnp.bfloat16),
            fresh_k_ref[:, lanes],
            across,
            preferred_element_type=jnp.float32,
        )
        score_ref[:, cached_len:] = own
        scores = jnp.where(valid_ref[...] > 0.0, score_ref[...] * factor, MASKED)
        highest = jnp.max(scores, axis=1, keepdims=True)
        weights = jnp.exp(scores - highest)
        totals = jnp.sum(weights, axis=1, keepdims=True)
        weights_b = weights.astype(jnp.bfloat16)
        score_ref[...] = weights_b.astype(jnp.float32)
        own_mixed = jnp.dot(
            weights_b[:, cached_len:], fresh_v_ref[:, lanes], preferred_element_type=jnp.float32
        )
        for r in range(requests):
            here = slice(r * group_size, (r + 1) * group_size)
            mixed_ref[here, :] = jnp.dot(
                score_ref[here, :cached_len].astype(jnp.bfloat16),
                value_ref[r, :, lanes],
                preferred_element_type=jnp.float32,
            )
        mixed_ref[...] = (mixed_ref[...] + own_mixed) / totals
        for h in range(group_size):
            at = (j * group_size + h) * HEAD_SIZE
            out_ref[:, at : at + HEAD_SIZE] = mixed_ref[
                pl.ds(h, requests, stride=group_size), :
            ].astype(jnp.bfloat16)


def attend(heads, valid, routing_b, key_cache, value_cache, new_key, new_value, returned):
    requests, cached_len, _ = key_cache.shape
    cached_count, rows, _ = heads.shape
    features = cached_count * rows // requests * HEAD_SIZE
    return pl.pallas_call(
        functools.partial(attend_kernel, len(returned)),
        out_shape=jax.ShapeDtypeStruct((requests, features), jnp.bfloat16),
        in_specs=[VMEM] * (7 + len(returned)),
        out_specs=VMEM,
        scratch_shapes=[
            pltpu.VMEM((rows, HEAD_SIZE), jnp.float32),
            pltpu.VMEM((rows, cached_len + requests), jnp.float32),
            pltpu.VMEM((rows, HEAD_SIZE), jnp.float32),
        ],
        compiler_params=grant(20),
        name="attend",
    )(heads, valid, routing_b, key_cache, value_cache, new_key, new_value, *returned)


def after(arrays, *tokens):
    return lax.optimization_barrier((tuple(arrays), tokens))[0]


def shards(
    hidden,
    base_query,
    key_cache,
    value_cache,
    new_key,
    new_value,
    lengths,
    request_adapter,
    adapter_store_row,
    adapter_down,
    adapter_up,
):
    request_rows = hidden.shape[0]
    pool_count = lax.axis_size("pool")
    tp_count = lax.axis_size("tp")
    capacity = max(2, 2 * request_rows // pool_count)
    owned_count = adapter_down.shape[0]
    step_count = pool_count // tp_count
    per_group = max(1, ROWS // capacity)
    group_count = step_count // per_group
    adapter_down = jnp.swapaxes(adapter_down, 1, 2)

    def move(g, rows):
        parts = []
        for k in range(per_group):
            step = g * per_group + k
            part = rows
            if per_group > 1:
                part = lax.slice_in_dim(rows, k * capacity, (k + 1) * capacity, axis=rows.ndim - 2)
            pairs = [
                (i * tp_count + c, (i ^ (tp_count * step + c)) * tp_count + c)
                for i in range(pool_count)
                for c in range(tp_count)
            ]
            parts.append(lax.ppermute(part, ("pool", "tp"), pairs))
        return parts[0] if per_group == 1 else jnp.concatenate(parts, axis=rows.ndim - 2)

    def swap(array):
        return lax.ppermute(array, "tp", [(0, 1), (1, 0)])

    *groups, routing_b = pack(
        hidden, request_adapter, adapter_store_row, pool_count, tp_count, capacity, owned_count, per_group * capacity
    )
    factors = [adapter_down, swap(adapter_down), adapter_up, swap(adapter_up)]
    heads, valid, factors[0], factors[2], key_cache, value_cache = prepare(
        *after([base_query, lengths, adapter_down, adapter_up, key_cache, value_cache], routing_b)
    )
    near = list(range(group_count // 2))
    far = list(range(group_count // 2, group_count))
    arrived = {g: move(g, groups[g]) for g in far + near}
    returned = {}
    for chosen in (near, *[[g] for g in far]):
        served = serve([arrived[g] for g in chosen], factors)
        returned |= {g: move(g, rows) for g, rows in zip(chosen, served)}
    returned = [returned[g] for g in range(group_count)]
    others = [swap(rows) for rows in returned]
    return attend(
        heads, valid, routing_b, key_cache, value_cache, new_key, new_value, returned + others
    )


def solution(mesh):
    placed = (
        P(("rep", "pool"), None),
        P(("rep", "pool"), "tp"),
        P(("rep", "pool"), None, "tp"),
        P(("rep", "pool"), None, "tp"),
        P(("rep", "pool"), "tp"),
        P(("rep", "pool"), "tp"),
        P(("rep", "pool")),
        P(("rep", "pool")),
        P("rep"),
        P("pool", "tp", None),
        P("pool", None, "tp"),
    )
    return jax.shard_map(
        shards, mesh=mesh, in_specs=placed, out_specs=P(("rep", "pool"), "tp"), check_vma=False
    )
```

```python
import functools
import math

import jax
import jax.numpy as jnp
from jax import lax
from jax.experimental import pallas as pl
from jax.experimental.pallas import tpu as pltpu
from jax.sharding import PartitionSpec as P

HEAD_SIZE = 128
ADAPTER_SCALE = 2.0
MASKED = -1e30
FACTOR = 1.0 / math.sqrt(HEAD_SIZE)
LANES = 128
ROWS = 16
MIB = 1024 * 1024

VMEM = pl.BlockSpec(memory_space=pltpu.VMEM)
ANYWHERE = pl.BlockSpec(memory_space=pl.ANY)


def grant(mib):
    return pltpu.CompilerParams(vmem_limit_bytes=mib * MIB)


def column_of(row):
    count = row.shape[1]
    here = lax.broadcasted_iota(jnp.int32, (count, count), 0)
    there = lax.broadcasted_iota(jnp.int32, (count, count), 1)
    spread = jnp.broadcast_to(row, (count, count))
    return jnp.sum(jnp.where(here == there, spread, 0), axis=1, keepdims=True)


def in_hbm(array):
    return pltpu.with_memory_space_constraint(array, pltpu.HBM)


def as_bf16(mask):
    return mask.astype(jnp.float32).astype(jnp.bfloat16)


def pack_kernel(pool_count, tp_count, capacity, owned_count, adapter_hbm, store_hbm, hidden_hbm, *refs):
    *outs, routing_ref, place_ref, held_ref, adapter_ref, store_ref, sems, index_sems = refs
    chunks = sems.shape[0]
    step = held_ref.shape[1] // chunks
    small = [
        pltpu.make_async_copy(adapter_hbm, adapter_ref, index_sems.at[0]),
        pltpu.make_async_copy(store_hbm, store_ref, index_sems.at[1]),
    ]
    copies = [
        pltpu.make_async_copy(
            hidden_hbm.at[:, pl.ds(c * step, step)], held_ref.at[:, pl.ds(c * step, step)], sems.at[c]
        )
        for c in range(chunks)
    ]
    for copy in small + copies:
        copy.start()
    for copy in small:
        copy.wait()
    adapters = store_ref.shape[1]
    requests = adapter_ref.shape[1]
    slot_total = pool_count // tp_count * capacity
    matches = lax.broadcasted_iota(jnp.int32, (adapters, requests), 0) == adapter_ref[...]
    position = jnp.sum(jnp.where(matches, column_of(store_ref[...]), 0), axis=0, keepdims=True)
    owner = lax.div(position, jnp.int32(owned_count))
    held = position - owner * owned_count
    distance = lax.bitwise_xor(owner, jnp.broadcast_to(lax.axis_index("pool"), owner.shape))
    step_of = lax.div(distance, jnp.int32(tp_count))
    mine = distance - step_of * tp_count == lax.axis_index("tp")
    earlier = lax.broadcasted_iota(jnp.int32, (requests, requests), 0) < lax.broadcasted_iota(
        jnp.int32, (requests, requests), 1
    )
    same = column_of(owner) == owner
    rank = jnp.sum(jnp.where(same & earlier, 1, 0), axis=0, keepdims=True)
    target = step_of * capacity + rank + jnp.where(mine, 0, slot_total)
    place_ref[0:1, :] = target
    place_ref[1:2, :] = held
    for copy in copies:
        copy.wait()
    pack_rows(target, held, held_ref, slot_total // 2, outs)
    back = lax.broadcasted_iota(jnp.int32, (requests, tp_count * slot_total), 1) == column_of(target)
    routing_ref[...] = as_bf16(back)


def pack_rows(target, held, held_ref, first, outs):
    width = held_ref.shape[1]
    requests = held_ref.shape[0]
    count = sum(out.shape[0] for out in outs)
    routing = lax.broadcasted_iota(jnp.int32, (count, requests), 0) + first == target
    held_slot = jnp.sum(jnp.where(routing, held, 0), axis=1, keepdims=True)
    tags = jnp.broadcast_to(held_slot, (count, LANES)).astype(jnp.float32).astype(jnp.bfloat16)
    routing_b = as_bf16(routing)
    chunks = 4
    step = width // chunks
    for c in range(chunks):
        columns = slice(c * step, (c + 1) * step)
        packed = jnp.dot(
            routing_b, held_ref[:, columns], preferred_element_type=jnp.float32
        ).astype(jnp.bfloat16)
        for g, out in enumerate(outs):
            out[:, columns] = packed[g * out.shape[0] : (g + 1) * out.shape[0]]
    for g, out in enumerate(outs):
        out[:, width:] = tags[g * out.shape[0] : (g + 1) * out.shape[0]]


def pack_near_kernel(place_ref, held_ref, *outs):
    pack_rows(place_ref[0:1, :], place_ref[1:2, :], held_ref, 0, outs)


def pack(hidden, request_adapter, adapter_store_row, pool_count, tp_count, capacity, owned_count, group_rows):
    requests, width = hidden.shape
    adapters = adapter_store_row.shape[0]
    slot_total = pool_count // tp_count * capacity
    group_count = slot_total // group_rows // 2
    chunks = 4
    rows = [pltpu.VMEM((group_rows, width + LANES), jnp.bfloat16)] * group_count
    *far, routing_b, place, held = pl.pallas_call(
        functools.partial(pack_kernel, pool_count, tp_count, capacity, owned_count),
        out_shape=rows
        + [
            pltpu.VMEM((requests, tp_count * slot_total), jnp.bfloat16),
            pltpu.VMEM((2, requests), jnp.int32),
            pltpu.VMEM((requests, width), jnp.bfloat16),
        ],
        in_specs=[ANYWHERE] * 3,
        out_specs=[VMEM] * (group_count + 3),
        scratch_shapes=[
            pltpu.VMEM((1, requests), jnp.int32),
            pltpu.VMEM((1, adapters), jnp.int32),
            pltpu.SemaphoreType.DMA((chunks,)),
            pltpu.SemaphoreType.DMA((2,)),
        ],
        compiler_params=grant(8),
        name="pack",
    )(
        in_hbm(request_adapter.reshape(1, requests)),
        in_hbm(adapter_store_row.reshape(1, adapters)),
        in_hbm(hidden),
    )
    return far, routing_b, place, held


def pack_near(place, held, like):
    return pl.pallas_call(
        pack_near_kernel,
        out_shape=[pltpu.VMEM(row.shape, row.dtype) for row in like],
        in_specs=[VMEM] * 2,
        out_specs=[VMEM] * len(like),
        compiler_params=grant(8),
        name="pack_near",
    )(place, held)


def serve_kernel(count, parts, *refs):
    rows, (down_ref, down_far_ref, up_ref, up_far_ref), outs = (
        refs[:count],
        refs[count : count + 4],
        refs[count + 4 :],
    )
    owned_count, rank, width = down_ref.shape
    here = lax.axis_index("tp")
    there = 1 - here
    tags = jnp.concatenate([row[:, 2 * width : 2 * width + 1] for row in rows], axis=0)
    tags = tags.astype(jnp.float32)
    middle = jnp.zeros((tags.shape[0], rank), jnp.float32)
    for half, factors in ((here, down_ref), (there, down_far_ref)):
        columns = pl.ds(pl.multiple_of(half * width, LANES), width)
        features = jnp.concatenate([row[:, columns] for row in rows], axis=0)
        for slot in range(owned_count):
            partial = lax.dot_general(
                features,
                factors[slot],
                (((1,), (1,)), ((), ())),
                preferred_element_type=jnp.float32,
            )
            middle = middle + jnp.where(tags == float(slot), partial, 0.0)
    middle = middle.astype(jnp.bfloat16).astype(jnp.float32)
    chosen = jnp.concatenate(
        [jnp.where(tags == float(slot), middle, 0.0) for slot in range(owned_count)], axis=1
    ).astype(jnp.bfloat16)
    step = min(width, 1024)
    for half, factors in ((here, up_ref), (there, up_far_ref)):
        for c in range(width // step):
            columns = slice(c * step, (c + 1) * step)
            stacked = jnp.concatenate([factors[slot, :, columns] for slot in range(owned_count)], axis=0)
            total = jnp.dot(chosen, stacked, preferred_element_type=jnp.float32)
            total = (ADAPTER_SCALE * total).astype(jnp.bfloat16)
            at = 0
            for k in range(len(rows)):
                part, column = divmod(c * step, width // parts)
                out = outs[k * parts + part]
                out[half, :, column : column + step] = total[at : at + out.shape[1]]
                at += out.shape[1]


def serve(rows, factors, parts=1):
    width = factors[0].shape[2]
    return pl.pallas_call(
        functools.partial(serve_kernel, len(rows), parts),
        out_shape=[
            pltpu.VMEM((2, row.shape[0], width // parts), jnp.bfloat16) for row in rows for _ in range(parts)
        ],
        in_specs=[VMEM] * (len(rows) + 4),
        out_specs=[VMEM] * (len(rows) * parts),
        compiler_params=grant(8),
        name="serve",
    )(*rows, *factors)


def prepare_kernel(
    base_hbm,
    lengths_hbm,
    fresh_k_hbm,
    fresh_v_hbm,
    down_hbm,
    up_hbm,
    key_hbm,
    value_hbm,
    heads_ref,
    score_ref,
    fresh_k_ref,
    fresh_v_ref,
    down_ref,
    up_ref,
    key_ref,
    value_ref,
    base_in,
    lengths_in,
    fresh_k_in,
    fresh_v_in,
    sems,
):
    pairs = [
        (lengths_hbm, lengths_in),
        (base_hbm, base_in),
        (fresh_k_hbm, fresh_k_in),
        (fresh_v_hbm, fresh_v_in),
        (key_hbm, key_ref),
        (down_hbm, down_ref),
        (up_hbm, up_ref),
        (value_hbm, value_ref),
    ]
    copies = [pltpu.make_async_copy(*pair, sems.at[i]) for i, pair in enumerate(pairs)]
    for copy in copies:
        copy.start()
    for copy in copies[:4]:
        copy.wait()
    requests = base_in.shape[0]
    cached_count, rows, _ = heads_ref.shape
    group_size = rows // requests
    for j in range(cached_count):
        lanes = slice(j * HEAD_SIZE, (j + 1) * HEAD_SIZE)
        for h in range(group_size):
            at = (j * group_size + h) * HEAD_SIZE
            here = pl.ds(h, requests, stride=group_size)
            heads_ref[j, here, :] = base_in[:, at : at + HEAD_SIZE].astype(jnp.float32)
            fresh_k_ref[j, here, :] = fresh_k_in[:, lanes].astype(jnp.float32)
            fresh_v_ref[j, here, :] = fresh_v_in[:, lanes].astype(jnp.float32)
    pair_count, places, _ = key_ref.shape
    cached_len = places * pair_count // requests
    side = requests // pair_count
    request = lax.broadcasted_iota(jnp.int32, (requests, places), 0)
    place = lax.broadcasted_iota(jnp.int32, (requests, places), 1)
    place = place - lax.rem(request, jnp.int32(side)) * cached_len
    allowed = (place >= 0) & (place < column_of(lengths_in[...]))
    allowed = allowed.astype(jnp.float32)
    for h in range(group_size):
        score_ref[0, pl.ds(h, requests, stride=group_size), :] = allowed
    valid = score_ref[0] > 0.0
    copies[4].wait()
    block = side * group_size
    for j in range(cached_count):
        lanes = slice(j * HEAD_SIZE, (j + 1) * HEAD_SIZE)
        for p in range(pair_count):
            here = slice(p * block, (p + 1) * block)
            score_ref[j, here, :] = lax.dot_general(
                heads_ref[j, here, :].astype(jnp.bfloat16),
                key_ref[p, :, lanes],
                (((1,), (1,)), ((), ())),
                preferred_element_type=jnp.float32,
            )
        score_ref[j] = jnp.where(valid, score_ref[j] * FACTOR, MASKED)
    for copy in copies[5:]:
        copy.wait()


def prepare(base_query, lengths, new_key, new_value, adapter_down, adapter_up, key_cache, value_cache):
    requests, features = base_query.shape
    cached_count = new_key.shape[1] // HEAD_SIZE
    rows = requests * features // (HEAD_SIZE * cached_count)
    places = key_cache.shape[1]
    held = [adapter_down, adapter_up, key_cache, value_cache]
    moved = [base_query, lengths.reshape(1, requests), new_key, new_value]
    return pl.pallas_call(
        prepare_kernel,
        out_shape=[
            pltpu.VMEM((cached_count, rows, HEAD_SIZE), jnp.float32),
            pltpu.VMEM((cached_count, rows, places), jnp.float32),
            pltpu.VMEM((cached_count, rows, HEAD_SIZE), jnp.float32),
            pltpu.VMEM((cached_count, rows, HEAD_SIZE), jnp.float32),
        ]
        + [pltpu.VMEM(array.shape, array.dtype) for array in held],
        in_specs=[ANYWHERE] * 8,
        out_specs=[VMEM] * 8,
        scratch_shapes=[pltpu.VMEM(array.shape, array.dtype) for array in moved]
        + [pltpu.SemaphoreType.DMA((8,))],
        compiler_params=grant(8),
        cost_estimate=pl.CostEstimate(
            flops=0, bytes_accessed=4 * key_cache.size + 4 * adapter_up.size, transcendentals=0
        ),
        name="prepare",
    )(*[in_hbm(array) for array in moved + held])


def attend_kernel(
    first,
    counts,
    heads_ref,
    score_ref,
    fresh_k_ref,
    fresh_v_ref,
    key_ref,
    value_ref,
    routing_ref,
    *refs,
):
    count = len(counts)
    returned = refs[:count]
    out_hbm, delta_ref, weight_ref, mixed_ref, out_ref, sems = refs[-6:]
    pair_count, _, _ = key_ref.shape
    _, rows, _ = heads_ref.shape
    requests = out_hbm.shape[0]
    group_size = rows // requests
    block = rows // pair_count
    half = lax.axis_index("tp")
    width = group_size * HEAD_SIZE
    copies = []
    for k in range(out_ref.shape[0]):
        j = first + k
        lanes = slice(j * HEAD_SIZE, (j + 1) * HEAD_SIZE)
        arrived = jnp.concatenate(
            [piece[half, :, (j - at) * width : (j - at + 1) * width] for piece, at in zip(returned, counts)],
            axis=0,
        )
        delta = jnp.dot(routing_ref[...], arrived, preferred_element_type=jnp.float32)
        for h in range(group_size):
            delta_ref[pl.ds(h, requests, stride=group_size), :] = delta[
                :, h * HEAD_SIZE : (h + 1) * HEAD_SIZE
            ]
        for p in range(pair_count):
            here = slice(p * block, (p + 1) * block)
            weight_ref[here, :] = lax.dot_general(
                delta_ref[here, :].astype(jnp.bfloat16),
                key_ref[p, :, lanes],
                (((1,), (1,)), ((), ())),
                preferred_element_type=jnp.float32,
            )
        scores = score_ref[j] + weight_ref[...] * FACTOR
        own = (heads_ref[j] + delta_ref[...]) * fresh_k_ref[j]
        own = jnp.sum(own, axis=1, keepdims=True) * FACTOR
        highest = jnp.maximum(jnp.max(scores, axis=1, keepdims=True), own)
        weights = jnp.exp(scores - highest)
        own_weight = jnp.exp(own - highest)
        totals = jnp.sum(weights, axis=1, keepdims=True) + own_weight
        weight_ref[...] = weights
        own_b = own_weight.astype(jnp.bfloat16).astype(jnp.float32)
        for p in range(pair_count):
            here = slice(p * block, (p + 1) * block)
            mixed_ref[here, :] = jnp.dot(
                weight_ref[here, :].astype(jnp.bfloat16),
                value_ref[p, :, lanes],
                preferred_element_type=jnp.float32,
            )
        mixed_ref[...] = (mixed_ref[...] + own_b * fresh_v_ref[j]) / totals
        for h in range(group_size):
            out_ref[k, :, h * HEAD_SIZE : (h + 1) * HEAD_SIZE] = mixed_ref[
                pl.ds(h, requests, stride=group_size), :
            ].astype(jnp.bfloat16)
        copy = pltpu.make_async_copy(
            out_ref.at[k], out_hbm.at[:, pl.ds(j * width, width)], sems.at[k]
        )
        copy.start()
        copies.append(copy)
    for copy in copies:
        copy.wait()


def attend(held, routing_b, returned, first, span, counts, out=None):
    cached_count, rows, _ = held[0].shape
    requests = routing_b.shape[0]
    width = rows // requests * HEAD_SIZE
    operands = [*held, routing_b, *returned]
    aliases = {}
    if out is not None:
        aliases = {len(operands): 0}
        operands.append(out)
    return pl.pallas_call(
        functools.partial(attend_kernel, first, counts),
        out_shape=jax.ShapeDtypeStruct((requests, cached_count * width), jnp.bfloat16),
        in_specs=[VMEM] * (len(held) + 1 + len(returned)) + [ANYWHERE] * len(aliases),
        out_specs=ANYWHERE,
        input_output_aliases=aliases,
        scratch_shapes=[
            pltpu.VMEM((rows, HEAD_SIZE), jnp.float32),
            pltpu.VMEM((rows, held[1].shape[2]), jnp.float32),
            pltpu.VMEM((rows, HEAD_SIZE), jnp.float32),
            pltpu.VMEM((span, requests, width), jnp.bfloat16),
            pltpu.SemaphoreType.DMA((span,)),
        ],
        compiler_params=grant(8),
        name="attend",
    )(*operands)


def after(arrays, *tokens):
    return lax.optimization_barrier((tuple(arrays), tokens))[0]


def shards(
    hidden,
    base_query,
    key_cache,
    value_cache,
    new_key,
    new_value,
    lengths,
    request_adapter,
    adapter_store_row,
    adapter_down,
    adapter_up,
):
    request_rows = hidden.shape[0]
    pool_count = lax.axis_size("pool")
    tp_count = lax.axis_size("tp")
    capacity = max(2, 2 * request_rows // pool_count)
    owned_count = adapter_down.shape[0]
    step_count = pool_count // tp_count
    per_group = max(1, ROWS // capacity)
    group_count = step_count // per_group
    adapter_down = jnp.swapaxes(adapter_down, 1, 2)

    def move(g, rows):
        parts = []
        for k in range(per_group):
            step = g * per_group + k
            part = rows
            if per_group > 1:
                part = lax.slice_in_dim(rows, k * capacity, (k + 1) * capacity, axis=rows.ndim - 2)
            pairs = [
                (i * tp_count + c, (i ^ (tp_count * step + c)) * tp_count + c)
                for i in range(pool_count)
                for c in range(tp_count)
            ]
            parts.append(lax.ppermute(part, ("pool", "tp"), pairs))
        return parts[0] if per_group == 1 else jnp.concatenate(parts, axis=rows.ndim - 2)

    def swap(array):
        return lax.ppermute(array, "tp", [(0, 1), (1, 0)])

    far_rows, routing_b, place, spread = pack(
        hidden, request_adapter, adapter_store_row, pool_count, tp_count, capacity, owned_count, per_group * capacity
    )
    factors = [adapter_down, swap(adapter_down), adapter_up, swap(adapter_up)]
    cached_len, features = key_cache.shape[1:]
    pairs = (request_rows // 2, 2 * cached_len, features)
    *held, factors[0], factors[2], key_cache, value_cache = prepare(
        *after(
            [
                base_query,
                lengths,
                new_key,
                new_value,
                adapter_down,
                adapter_up,
                key_cache.reshape(pairs),
                value_cache.reshape(pairs),
            ],
            routing_b,
        )
    )
    held = [*held, key_cache, value_cache]
    *far, last = list(range(group_count // 2, group_count))
    near = list(range(group_count // 2))
    ready = after([place, spread], factors[1], factors[3])
    groups = [*pack_near(*ready, far_rows), *far_rows]
    arrived = {g: move(g, groups[g]) for g in [*far, last, *near]}
    early = serve([arrived[g] for g in far], factors)
    served = serve(after([arrived[g] for g in near], early[0]), factors)
    returned = {g: move(g, rows) for g, rows in zip(near, served)}
    returned |= {g: move(g, rows) for g, rows in zip(far, after(early, served[0]))}
    final = serve(after([arrived[last]], served[0]), factors, parts=2)
    final = [move(last, rows) for rows in final]
    whole = [returned[g] for g in range(last)]
    others = [swap(rows) for rows in whole]
    cached_count = features // HEAD_SIZE
    span = cached_count // len(final)
    out = None
    for k, rows in enumerate(final):
        first = k * span
        pieces = [*whole, rows, *others, swap(rows)]
        counts = [*[0] * last, first] * 2
        out = attend(held, routing_b, pieces, first, span, counts, out)
    return out


def solution(mesh):
    placed = (
        P(("rep", "pool"), None),
        P(("rep", "pool"), "tp"),
        P(("rep", "pool"), None, "tp"),
        P(("rep", "pool"), None, "tp"),
        P(("rep", "pool"), "tp"),
        P(("rep", "pool"), "tp"),
        P(("rep", "pool")),
        P(("rep", "pool")),
        P("rep"),
        P("pool", "tp", None),
        P("pool", None, "tp"),
    )
    return jax.shard_map(
        shards, mesh=mesh, in_specs=placed, out_specs=P(("rep", "pool"), "tp"), check_vma=False
    )
```

```python
import functools
import math

import jax
import jax.numpy as jnp
from jax import lax
from jax.experimental import pallas as pl
from jax.experimental.pallas import tpu as pltpu
from jax.sharding import PartitionSpec as P

HEAD_SIZE = 128
ADAPTER_SCALE = 2.0
MASKED = -1e30
FACTOR = 1.0 / math.sqrt(HEAD_SIZE)
LANES = 128
ROWS = 16
MIB = 1024 * 1024

VMEM = pl.BlockSpec(memory_space=pltpu.VMEM)
ANYWHERE = pl.BlockSpec(memory_space=pl.ANY)


def grant(mib):
    return pltpu.CompilerParams(vmem_limit_bytes=mib * MIB)


def column_of(row):
    count = row.shape[1]
    here = lax.broadcasted_iota(jnp.int32, (count, count), 0)
    there = lax.broadcasted_iota(jnp.int32, (count, count), 1)
    spread = jnp.broadcast_to(row, (count, count))
    return jnp.sum(jnp.where(here == there, spread, 0), axis=1, keepdims=True)


def in_hbm(array):
    return pltpu.with_memory_space_constraint(array, pltpu.HBM)


def as_bf16(mask):
    return mask.astype(jnp.float32).astype(jnp.bfloat16)


def pack_kernel(pool_count, tp_count, capacity, owned_count, adapter_hbm, store_hbm, hidden_hbm, *refs):
    *outs, routing_ref, place_ref, held_ref, adapter_ref, store_ref, sems, index_sems = refs
    chunks = sems.shape[0]
    step = held_ref.shape[1] // chunks
    small = [
        pltpu.make_async_copy(adapter_hbm, adapter_ref, index_sems.at[0]),
        pltpu.make_async_copy(store_hbm, store_ref, index_sems.at[1]),
    ]
    copies = [
        pltpu.make_async_copy(
            hidden_hbm.at[:, pl.ds(c * step, step)], held_ref.at[:, pl.ds(c * step, step)], sems.at[c]
        )
        for c in range(chunks)
    ]
    for copy in small + copies:
        copy.start()
    for copy in small:
        copy.wait()
    adapters = store_ref.shape[1]
    requests = adapter_ref.shape[1]
    slot_total = pool_count // tp_count * capacity
    matches = lax.broadcasted_iota(jnp.int32, (adapters, requests), 0) == adapter_ref[...]
    position = jnp.sum(jnp.where(matches, column_of(store_ref[...]), 0), axis=0, keepdims=True)
    owner = lax.div(position, jnp.int32(owned_count))
    held = position - owner * owned_count
    distance = lax.bitwise_xor(owner, jnp.broadcast_to(lax.axis_index("pool"), owner.shape))
    step_of = lax.div(distance, jnp.int32(tp_count))
    mine = distance - step_of * tp_count == lax.axis_index("tp")
    earlier = lax.broadcasted_iota(jnp.int32, (requests, requests), 0) < lax.broadcasted_iota(
        jnp.int32, (requests, requests), 1
    )
    same = column_of(owner) == owner
    rank = jnp.sum(jnp.where(same & earlier, 1, 0), axis=0, keepdims=True)
    target = step_of * capacity + rank + jnp.where(mine, 0, slot_total)
    place_ref[0:1, :] = target
    place_ref[1:2, :] = held
    for copy in copies:
        copy.wait()
    pack_rows(target, held, held_ref, slot_total // 2, outs)
    back = lax.broadcasted_iota(jnp.int32, (requests, tp_count * slot_total), 1) == column_of(target)
    routing_ref[...] = as_bf16(back)


def pack_rows(target, held, held_ref, first, outs):
    width = held_ref.shape[1]
    requests = held_ref.shape[0]
    count = sum(out.shape[0] for out in outs)
    routing = lax.broadcasted_iota(jnp.int32, (count, requests), 0) + first == target
    held_slot = jnp.sum(jnp.where(routing, held, 0), axis=1, keepdims=True)
    tags = jnp.broadcast_to(held_slot, (count, LANES)).astype(jnp.float32).astype(jnp.bfloat16)
    routing_b = as_bf16(routing)
    chunks = 4
    step = width // chunks
    for c in range(chunks):
        columns = slice(c * step, (c + 1) * step)
        packed = jnp.dot(
            routing_b, held_ref[:, columns], preferred_element_type=jnp.float32
        ).astype(jnp.bfloat16)
        for g, out in enumerate(outs):
            out[:, columns] = packed[g * out.shape[0] : (g + 1) * out.shape[0]]
    for g, out in enumerate(outs):
        out[:, width:] = tags[g * out.shape[0] : (g + 1) * out.shape[0]]


def pack_near_kernel(place_ref, held_ref, *outs):
    pack_rows(place_ref[0:1, :], place_ref[1:2, :], held_ref, 0, outs)


def pack(hidden, request_adapter, adapter_store_row, pool_count, tp_count, capacity, owned_count, group_rows):
    requests, width = hidden.shape
    adapters = adapter_store_row.shape[0]
    slot_total = pool_count // tp_count * capacity
    group_count = slot_total // group_rows // 2
    chunks = 4
    rows = [pltpu.VMEM((group_rows, width + LANES), jnp.bfloat16)] * group_count
    *far, routing_b, place, held = pl.pallas_call(
        functools.partial(pack_kernel, pool_count, tp_count, capacity, owned_count),
        out_shape=rows
        + [
            pltpu.VMEM((requests, tp_count * slot_total), jnp.bfloat16),
            pltpu.VMEM((2, requests), jnp.int32),
            pltpu.VMEM((requests, width), jnp.bfloat16),
        ],
        in_specs=[ANYWHERE] * 3,
        out_specs=[VMEM] * (group_count + 3),
        scratch_shapes=[
            pltpu.VMEM((1, requests), jnp.int32),
            pltpu.VMEM((1, adapters), jnp.int32),
            pltpu.SemaphoreType.DMA((chunks,)),
            pltpu.SemaphoreType.DMA((2,)),
        ],
        compiler_params=grant(8),
        name="pack",
    )(
        in_hbm(request_adapter.reshape(1, requests)),
        in_hbm(adapter_store_row.reshape(1, adapters)),
        in_hbm(hidden),
    )
    return far, routing_b, place, held


def pack_near(place, held, like):
    return pl.pallas_call(
        pack_near_kernel,
        out_shape=[pltpu.VMEM(row.shape, row.dtype) for row in like],
        in_specs=[VMEM] * 2,
        out_specs=[VMEM] * len(like),
        compiler_params=grant(8),
        name="pack_near",
    )(place, held)


def serve_kernel(count, parts, *refs):
    rows, (down_ref, down_far_ref, up_ref, up_far_ref), outs = (
        refs[:count],
        refs[count : count + 4],
        refs[count + 4 :],
    )
    owned_count, rank, width = down_ref.shape
    here = lax.axis_index("tp")
    there = 1 - here
    tags = jnp.concatenate([row[:, 2 * width : 2 * width + 1] for row in rows], axis=0)
    tags = tags.astype(jnp.float32)
    middle = jnp.zeros((tags.shape[0], rank), jnp.float32)
    for half, factors in ((here, down_ref), (there, down_far_ref)):
        columns = pl.ds(pl.multiple_of(half * width, LANES), width)
        features = jnp.concatenate([row[:, columns] for row in rows], axis=0)
        for slot in range(owned_count):
            partial = lax.dot_general(
                features,
                factors[slot],
                (((1,), (1,)), ((), ())),
                preferred_element_type=jnp.float32,
            )
            middle = middle + jnp.where(tags == float(slot), partial, 0.0)
    middle = middle.astype(jnp.bfloat16).astype(jnp.float32)
    chosen = jnp.concatenate(
        [jnp.where(tags == float(slot), middle, 0.0) for slot in range(owned_count)], axis=1
    ).astype(jnp.bfloat16)
    step = min(width, 1024)
    for half, factors in ((here, up_ref), (there, up_far_ref)):
        for c in range(width // step):
            columns = slice(c * step, (c + 1) * step)
            stacked = jnp.concatenate([factors[slot, :, columns] for slot in range(owned_count)], axis=0)
            total = jnp.dot(chosen, stacked, preferred_element_type=jnp.float32)
            total = (ADAPTER_SCALE * total).astype(jnp.bfloat16)
            at = 0
            for k in range(len(rows)):
                part, column = divmod(c * step, width // parts)
                out = outs[k * parts + part]
                out[half, :, column : column + step] = total[at : at + out.shape[1]]
                at += out.shape[1]


def serve(rows, factors, parts=1):
    width = factors[0].shape[2]
    return pl.pallas_call(
        functools.partial(serve_kernel, len(rows), parts),
        out_shape=[
            pltpu.VMEM((2, row.shape[0], width // parts), jnp.bfloat16) for row in rows for _ in range(parts)
        ],
        in_specs=[VMEM] * (len(rows) + 4),
        out_specs=[VMEM] * (len(rows) * parts),
        compiler_params=grant(8),
        name="serve",
    )(*rows, *factors)


def prepare_kernel(
    base_hbm,
    lengths_hbm,
    fresh_k_hbm,
    fresh_v_hbm,
    down_hbm,
    up_hbm,
    key_hbm,
    value_hbm,
    heads_ref,
    score_ref,
    fresh_k_ref,
    fresh_v_ref,
    turned_ref,
    down_ref,
    up_ref,
    value_ref,
    base_in,
    lengths_in,
    fresh_k_in,
    fresh_v_in,
    key_ref,
    sems,
):
    pairs = [
        (lengths_hbm, lengths_in),
        (base_hbm, base_in),
        (fresh_k_hbm, fresh_k_in),
        (fresh_v_hbm, fresh_v_in),
        (key_hbm, key_ref),
        (down_hbm, down_ref),
        (up_hbm, up_ref),
        (value_hbm, value_ref),
    ]
    copies = [pltpu.make_async_copy(*pair, sems.at[i]) for i, pair in enumerate(pairs)]
    for copy in copies:
        copy.start()
    for copy in copies[:4]:
        copy.wait()
    requests = base_in.shape[0]
    cached_count, rows, _ = heads_ref.shape
    group_size = rows // requests
    for j in range(cached_count):
        lanes = slice(j * HEAD_SIZE, (j + 1) * HEAD_SIZE)
        for h in range(group_size):
            at = (j * group_size + h) * HEAD_SIZE
            here = pl.ds(h, requests, stride=group_size)
            heads_ref[j, here, :] = base_in[:, at : at + HEAD_SIZE].astype(jnp.float32)
            fresh_k_ref[j, here, :] = fresh_k_in[:, lanes].astype(jnp.float32)
            fresh_v_ref[j, here, :] = fresh_v_in[:, lanes].astype(jnp.float32)
    pair_count, places, _ = key_ref.shape
    cached_len = places * pair_count // requests
    side = requests // pair_count
    request = lax.broadcasted_iota(jnp.int32, (requests, places), 0)
    place = lax.broadcasted_iota(jnp.int32, (requests, places), 1)
    place = place - lax.rem(request, jnp.int32(side)) * cached_len
    allowed = (place >= 0) & (place < column_of(lengths_in[...]))
    allowed = allowed.astype(jnp.float32)
    for h in range(group_size):
        score_ref[0, pl.ds(h, requests, stride=group_size), :] = allowed
    valid = score_ref[0] > 0.0
    copies[4].wait()
    block = side * group_size
    for j in range(cached_count):
        lanes = slice(j * HEAD_SIZE, (j + 1) * HEAD_SIZE)
        for p in range(pair_count):
            here = slice(p * block, (p + 1) * block)
            turned = key_ref[p, :, lanes].T
            turned_ref[j, p] = turned
            score_ref[j, here, :] = jnp.dot(
                heads_ref[j, here, :].astype(jnp.bfloat16), turned, preferred_element_type=jnp.float32
            )
        score_ref[j] = jnp.where(valid, score_ref[j] * FACTOR, MASKED)
    for copy in copies[5:]:
        copy.wait()


def prepare(base_query, lengths, new_key, new_value, adapter_down, adapter_up, key_cache, value_cache):
    requests, features = base_query.shape
    cached_count = new_key.shape[1] // HEAD_SIZE
    rows = requests * features // (HEAD_SIZE * cached_count)
    places = key_cache.shape[1]
    held = [adapter_down, adapter_up, value_cache]
    moved = [base_query, lengths.reshape(1, requests), new_key, new_value]
    return pl.pallas_call(
        prepare_kernel,
        out_shape=[
            pltpu.VMEM((cached_count, rows, HEAD_SIZE), jnp.float32),
            pltpu.VMEM((cached_count, rows, places), jnp.float32),
            pltpu.VMEM((cached_count, rows, HEAD_SIZE), jnp.float32),
            pltpu.VMEM((cached_count, rows, HEAD_SIZE), jnp.float32),
            pltpu.VMEM((cached_count, key_cache.shape[0], HEAD_SIZE, places), key_cache.dtype),
        ]
        + [pltpu.VMEM(array.shape, array.dtype) for array in held],
        in_specs=[ANYWHERE] * 8,
        out_specs=[VMEM] * 8,
        scratch_shapes=[pltpu.VMEM(array.shape, array.dtype) for array in [*moved, key_cache]]
        + [pltpu.SemaphoreType.DMA((8,))],
        compiler_params=grant(12),
        cost_estimate=pl.CostEstimate(
            flops=0, bytes_accessed=4 * key_cache.size + 4 * adapter_up.size, transcendentals=0
        ),
        name="prepare",
    )(*[in_hbm(array) for array in [*moved, adapter_down, adapter_up, key_cache, value_cache]])


def attend_kernel(
    parts,
    heads_ref,
    score_ref,
    fresh_k_ref,
    fresh_v_ref,
    key_ref,
    value_ref,
    routing_ref,
    *refs,
):
    returned = refs[:-6]
    out_hbm, delta_ref, weight_ref, mixed_ref, out_ref, sems = refs[-6:]
    _, pair_count, _, _ = key_ref.shape
    _, rows, _ = heads_ref.shape
    requests = out_hbm.shape[0]
    group_size = rows // requests
    block = rows // pair_count
    half = lax.axis_index("tp")
    width = group_size * HEAD_SIZE
    copies = []
    cached_count = out_ref.shape[0]
    for j in range(cached_count):
        lanes = slice(j * HEAD_SIZE, (j + 1) * HEAD_SIZE)
        arrived = []
        for piece in parts:
            part, at = divmod(j * len(piece), cached_count)
            at = at // len(piece) * width
            arrived.append(returned[piece[part]][half, :, at : at + width])
        arrived = jnp.concatenate(arrived, axis=0)
        delta = jnp.dot(routing_ref[...], arrived, preferred_element_type=jnp.float32)
        for h in range(group_size):
            delta_ref[pl.ds(h, requests, stride=group_size), :] = delta[
                :, h * HEAD_SIZE : (h + 1) * HEAD_SIZE
            ]
        for p in range(pair_count):
            here = slice(p * block, (p + 1) * block)
            weight_ref[here, :] = jnp.dot(
                delta_ref[here, :].astype(jnp.bfloat16), key_ref[j, p], preferred_element_type=jnp.float32
            )
        scores = score_ref[j] + weight_ref[...] * FACTOR
        own = (heads_ref[j] + delta_ref[...]) * fresh_k_ref[j]
        own = jnp.sum(own, axis=1, keepdims=True) * FACTOR
        highest = jnp.maximum(jnp.max(scores, axis=1, keepdims=True), own)
        weights = jnp.exp(scores - highest)
        own_weight = jnp.exp(own - highest)
        totals = jnp.sum(weights, axis=1, keepdims=True) + own_weight
        weight_ref[...] = weights
        own_b = own_weight.astype(jnp.bfloat16).astype(jnp.float32)
        for p in range(pair_count):
            here = slice(p * block, (p + 1) * block)
            mixed_ref[here, :] = jnp.dot(
                weight_ref[here, :].astype(jnp.bfloat16),
                value_ref[p, :, lanes],
                preferred_element_type=jnp.float32,
            )
        mixed_ref[...] = (mixed_ref[...] + own_b * fresh_v_ref[j]) / totals
        for h in range(group_size):
            out_ref[j, :, h * HEAD_SIZE : (h + 1) * HEAD_SIZE] = mixed_ref[
                pl.ds(h, requests, stride=group_size), :
            ].astype(jnp.bfloat16)
        copy = pltpu.make_async_copy(
            out_ref.at[j], out_hbm.at[:, pl.ds(j * width, width)], sems.at[j]
        )
        copy.start()
        copies.append(copy)
    for copy in copies:
        copy.wait()


def attend(held, routing_b, pieces):
    cached_count, rows, _ = held[0].shape
    requests = routing_b.shape[0]
    width = rows // requests * HEAD_SIZE
    parts, returned = [], []
    for piece in pieces:
        parts.append(list(range(len(returned), len(returned) + len(piece))))
        returned.extend(piece)
    return pl.pallas_call(
        functools.partial(attend_kernel, parts),
        out_shape=jax.ShapeDtypeStruct((requests, cached_count * width), jnp.bfloat16),
        in_specs=[VMEM] * (len(held) + 1 + len(returned)),
        out_specs=ANYWHERE,
        scratch_shapes=[
            pltpu.VMEM((rows, HEAD_SIZE), jnp.float32),
            pltpu.VMEM((rows, held[1].shape[2]), jnp.float32),
            pltpu.VMEM((rows, HEAD_SIZE), jnp.float32),
            pltpu.VMEM((cached_count, requests, width), jnp.bfloat16),
            pltpu.SemaphoreType.DMA((cached_count,)),
        ],
        compiler_params=grant(8),
        name="attend",
    )(*held, routing_b, *returned)


def after(arrays, *tokens):
    return lax.optimization_barrier((tuple(arrays), tokens))[0]


def shards(
    hidden,
    base_query,
    key_cache,
    value_cache,
    new_key,
    new_value,
    lengths,
    request_adapter,
    adapter_store_row,
    adapter_down,
    adapter_up,
):
    request_rows = hidden.shape[0]
    pool_count = lax.axis_size("pool")
    tp_count = lax.axis_size("tp")
    capacity = max(2, 2 * request_rows // pool_count)
    owned_count = adapter_down.shape[0]
    step_count = pool_count // tp_count
    per_group = max(1, ROWS // capacity)
    group_count = step_count // per_group
    adapter_down = jnp.swapaxes(adapter_down, 1, 2)

    def move(g, rows):
        parts = []
        for k in range(per_group):
            step = g * per_group + k
            part = rows
            if per_group > 1:
                part = lax.slice_in_dim(rows, k * capacity, (k + 1) * capacity, axis=rows.ndim - 2)
            pairs = [
                (i * tp_count + c, (i ^ (tp_count * step + c)) * tp_count + c)
                for i in range(pool_count)
                for c in range(tp_count)
            ]
            parts.append(lax.ppermute(part, ("pool", "tp"), pairs))
        return parts[0] if per_group == 1 else jnp.concatenate(parts, axis=rows.ndim - 2)

    def swap(array):
        return lax.ppermute(array, "tp", [(0, 1), (1, 0)])

    far_rows, routing_b, place, spread = pack(
        hidden, request_adapter, adapter_store_row, pool_count, tp_count, capacity, owned_count, per_group * capacity
    )
    factors = [adapter_down, swap(adapter_down), adapter_up, swap(adapter_up)]
    cached_len, features = key_cache.shape[1:]
    pairs = (request_rows // 2, 2 * cached_len, features)
    *held, factors[0], factors[2], value_cache = prepare(
        *after(
            [
                base_query,
                lengths,
                new_key,
                new_value,
                adapter_down,
                adapter_up,
                key_cache.reshape(pairs),
                value_cache.reshape(pairs),
            ],
            routing_b,
        )
    )
    held = [*held, value_cache]
    *far, last = list(range(group_count // 2, group_count))
    near = list(range(group_count // 2))
    ready = after([place, spread], factors[1], factors[3])
    groups = [*pack_near(*ready, far_rows), *far_rows]
    arrived = {g: move(g, groups[g]) for g in [*far, last, *near]}
    early = serve([arrived[g] for g in far], factors)
    served = serve(after([arrived[g] for g in near], early[0]), factors)
    returned = {g: move(g, rows) for g, rows in zip(near, served)}
    returned |= {g: move(g, rows) for g, rows in zip(far, after(early, served[0]))}
    final = serve(after([arrived[last]], served[0]), factors, parts=2)
    final = [move(last, rows) for rows in final]
    whole = [returned[g] for g in range(last)]
    others = [swap(rows) for rows in whole]
    mine = [[rows] for rows in whole] + [final]
    theirs = [[rows] for rows in others] + [[swap(rows) for rows in final]]
    return attend(held, routing_b, mine + theirs)


def solution(mesh):
    placed = (
        P(("rep", "pool"), None),
        P(("rep", "pool"), "tp"),
        P(("rep", "pool"), None, "tp"),
        P(("rep", "pool"), None, "tp"),
        P(("rep", "pool"), "tp"),
        P(("rep", "pool"), "tp"),
        P(("rep", "pool")),
        P(("rep", "pool")),
        P("rep"),
        P("pool", "tp", None),
        P("pool", None, "tp"),
    )
    return jax.shard_map(
        shards, mesh=mesh, in_specs=placed, out_specs=P(("rep", "pool"), "tp"), check_vma=False
    )
```

```python
import functools
import math

import jax
import jax.numpy as jnp
from jax import lax
from jax.experimental import pallas as pl
from jax.experimental.pallas import tpu as pltpu
from jax.sharding import PartitionSpec as P

HEAD_SIZE = 128
ADAPTER_SCALE = 2.0
MASKED = -1e30
FACTOR = 1.0 / math.sqrt(HEAD_SIZE)
LANES = 128
ROWS = 16
MIB = 1024 * 1024

VMEM = pl.BlockSpec(memory_space=pltpu.VMEM)
ANYWHERE = pl.BlockSpec(memory_space=pl.ANY)


def grant(mib):
    return pltpu.CompilerParams(vmem_limit_bytes=mib * MIB)


def column_of(row):
    count = row.shape[1]
    here = lax.broadcasted_iota(jnp.int32, (count, count), 0)
    there = lax.broadcasted_iota(jnp.int32, (count, count), 1)
    spread = jnp.broadcast_to(row, (count, count))
    return jnp.sum(jnp.where(here == there, spread, 0), axis=1, keepdims=True)


def in_hbm(array):
    return pltpu.with_memory_space_constraint(array, pltpu.HBM)


def as_bf16(mask):
    return mask.astype(jnp.float32).astype(jnp.bfloat16)


def pack_kernel(pool_count, tp_count, capacity, owned_count, adapter_hbm, store_hbm, hidden_hbm, *refs):
    *outs, routing_ref, place_ref, held_ref, adapter_ref, store_ref, sems, index_sems = refs
    chunks = sems.shape[0]
    step = held_ref.shape[1] // chunks
    small = [
        pltpu.make_async_copy(adapter_hbm, adapter_ref, index_sems.at[0]),
        pltpu.make_async_copy(store_hbm, store_ref, index_sems.at[1]),
    ]
    copies = [
        pltpu.make_async_copy(
            hidden_hbm.at[:, pl.ds(c * step, step)], held_ref.at[:, pl.ds(c * step, step)], sems.at[c]
        )
        for c in range(chunks)
    ]
    for copy in small + copies:
        copy.start()
    for copy in small:
        copy.wait()
    adapters = store_ref.shape[1]
    requests = adapter_ref.shape[1]
    slot_total = pool_count // tp_count * capacity
    matches = lax.broadcasted_iota(jnp.int32, (adapters, requests), 0) == adapter_ref[...]
    position = jnp.sum(jnp.where(matches, column_of(store_ref[...]), 0), axis=0, keepdims=True)
    owner = lax.div(position, jnp.int32(owned_count))
    held = position - owner * owned_count
    distance = lax.bitwise_xor(owner, jnp.broadcast_to(lax.axis_index("pool"), owner.shape))
    step_of = lax.div(distance, jnp.int32(tp_count))
    mine = distance - step_of * tp_count == lax.axis_index("tp")
    earlier = lax.broadcasted_iota(jnp.int32, (requests, requests), 0) < lax.broadcasted_iota(
        jnp.int32, (requests, requests), 1
    )
    same = column_of(owner) == owner
    rank = jnp.sum(jnp.where(same & earlier, 1, 0), axis=0, keepdims=True)
    target = step_of * capacity + rank + jnp.where(mine, 0, slot_total)
    place_ref[0:1, :] = target
    place_ref[1:2, :] = held
    for copy in copies:
        copy.wait()
    pack_rows(target, held, held_ref, slot_total // 2, outs)
    back = lax.broadcasted_iota(jnp.int32, (requests, tp_count * slot_total), 1) == column_of(target)
    routing_ref[...] = as_bf16(back)


def pack_rows(target, held, held_ref, first, outs):
    width = held_ref.shape[1]
    requests = held_ref.shape[0]
    count = sum(out.shape[0] for out in outs)
    routing = lax.broadcasted_iota(jnp.int32, (count, requests), 0) + first == target
    held_slot = jnp.sum(jnp.where(routing, held, 0), axis=1, keepdims=True)
    tags = jnp.broadcast_to(held_slot, (count, LANES)).astype(jnp.float32).astype(jnp.bfloat16)
    routing_b = as_bf16(routing)
    chunks = 4
    step = width // chunks
    for c in range(chunks):
        columns = slice(c * step, (c + 1) * step)
        packed = jnp.dot(
            routing_b, held_ref[:, columns], preferred_element_type=jnp.float32
        ).astype(jnp.bfloat16)
        for g, out in enumerate(outs):
            out[:, columns] = packed[g * out.shape[0] : (g + 1) * out.shape[0]]
    for g, out in enumerate(outs):
        out[:, width:] = tags[g * out.shape[0] : (g + 1) * out.shape[0]]


def pack_near_kernel(place_ref, held_ref, *outs):
    pack_rows(place_ref[0:1, :], place_ref[1:2, :], held_ref, 0, outs)


def pack(hidden, request_adapter, adapter_store_row, pool_count, tp_count, capacity, owned_count, group_rows):
    requests, width = hidden.shape
    adapters = adapter_store_row.shape[0]
    slot_total = pool_count // tp_count * capacity
    group_count = slot_total // group_rows // 2
    chunks = 4
    rows = [pltpu.VMEM((group_rows, width + LANES), jnp.bfloat16)] * group_count
    *far, routing_b, place, held = pl.pallas_call(
        functools.partial(pack_kernel, pool_count, tp_count, capacity, owned_count),
        out_shape=rows
        + [
            pltpu.VMEM((requests, tp_count * slot_total), jnp.bfloat16),
            pltpu.VMEM((2, requests), jnp.int32),
            pltpu.VMEM((requests, width), jnp.bfloat16),
        ],
        in_specs=[ANYWHERE] * 3,
        out_specs=[VMEM] * (group_count + 3),
        scratch_shapes=[
            pltpu.VMEM((1, requests), jnp.int32),
            pltpu.VMEM((1, adapters), jnp.int32),
            pltpu.SemaphoreType.DMA((chunks,)),
            pltpu.SemaphoreType.DMA((2,)),
        ],
        compiler_params=grant(8),
        name="pack",
    )(
        in_hbm(request_adapter.reshape(1, requests)),
        in_hbm(adapter_store_row.reshape(1, adapters)),
        in_hbm(hidden),
    )
    return far, routing_b, place, held


def pack_near(place, held, like):
    return pl.pallas_call(
        pack_near_kernel,
        out_shape=[pltpu.VMEM(row.shape, row.dtype) for row in like],
        in_specs=[VMEM] * 2,
        out_specs=[VMEM] * len(like),
        compiler_params=grant(8),
        name="pack_near",
    )(place, held)


def serve_kernel(count, parts, *refs):
    rows, (down_ref, down_far_ref, up_ref, up_far_ref), outs = (
        refs[:count],
        refs[count : count + 4],
        refs[count + 4 :],
    )
    owned_count, rank, width = down_ref.shape
    here = lax.axis_index("tp")
    there = 1 - here
    tags = jnp.concatenate([row[:, 2 * width : 2 * width + 1] for row in rows], axis=0)
    tags = tags.astype(jnp.float32)
    middle = jnp.zeros((tags.shape[0], rank), jnp.float32)
    for half, factors in ((here, down_ref), (there, down_far_ref)):
        columns = pl.ds(pl.multiple_of(half * width, LANES), width)
        features = jnp.concatenate([row[:, columns] for row in rows], axis=0)
        for slot in range(owned_count):
            partial = lax.dot_general(
                features,
                factors[slot],
                (((1,), (1,)), ((), ())),
                preferred_element_type=jnp.float32,
            )
            middle = middle + jnp.where(tags == float(slot), partial, 0.0)
    middle = middle.astype(jnp.bfloat16).astype(jnp.float32)
    chosen = jnp.concatenate(
        [jnp.where(tags == float(slot), middle, 0.0) for slot in range(owned_count)], axis=1
    ).astype(jnp.bfloat16)
    step = min(width, 1024)
    for half, factors in ((here, up_ref), (there, up_far_ref)):
        for c in range(width // step):
            columns = slice(c * step, (c + 1) * step)
            stacked = jnp.concatenate([factors[slot, :, columns] for slot in range(owned_count)], axis=0)
            total = jnp.dot(chosen, stacked, preferred_element_type=jnp.float32)
            total = (ADAPTER_SCALE * total).astype(jnp.bfloat16)
            at = 0
            for k in range(len(rows)):
                part, column = divmod(c * step, width // parts)
                out = outs[k * parts + part]
                out[half, :, column : column + step] = total[at : at + out.shape[1]]
                at += out.shape[1]


def serve(rows, factors, parts=1):
    width = factors[0].shape[2]
    return pl.pallas_call(
        functools.partial(serve_kernel, len(rows), parts),
        out_shape=[
            pltpu.VMEM((2, row.shape[0], width // parts), jnp.bfloat16) for row in rows for _ in range(parts)
        ],
        in_specs=[VMEM] * (len(rows) + 4),
        out_specs=[VMEM] * (len(rows) * parts),
        compiler_params=grant(8),
        name="serve",
    )(*rows, *factors)


def prepare_kernel(
    base_hbm,
    lengths_hbm,
    fresh_k_hbm,
    fresh_v_hbm,
    down_hbm,
    up_hbm,
    key_hbm,
    value_hbm,
    heads_ref,
    score_ref,
    fresh_k_ref,
    fresh_v_ref,
    turned_ref,
    down_ref,
    up_ref,
    value_ref,
    base_in,
    lengths_in,
    fresh_k_in,
    fresh_v_in,
    key_ref,
    sems,
):
    pairs = [
        (lengths_hbm, lengths_in),
        (base_hbm, base_in),
        (fresh_k_hbm, fresh_k_in),
        (fresh_v_hbm, fresh_v_in),
        (key_hbm, key_ref),
        (down_hbm, down_ref),
        (up_hbm, up_ref),
        (value_hbm, value_ref),
    ]
    copies = [pltpu.make_async_copy(*pair, sems.at[i]) for i, pair in enumerate(pairs)]
    for copy in copies:
        copy.start()
    for copy in copies[:4]:
        copy.wait()
    requests = base_in.shape[0]
    cached_count, rows, _ = heads_ref.shape
    group_size = rows // requests
    for j in range(cached_count):
        lanes = slice(j * HEAD_SIZE, (j + 1) * HEAD_SIZE)
        for h in range(group_size):
            at = (j * group_size + h) * HEAD_SIZE
            here = pl.ds(h, requests, stride=group_size)
            heads_ref[j, here, :] = base_in[:, at : at + HEAD_SIZE].astype(jnp.float32)
            fresh_k_ref[j, here, :] = fresh_k_in[:, lanes].astype(jnp.float32)
            fresh_v_ref[j, here, :] = fresh_v_in[:, lanes].astype(jnp.float32)
    pair_count, places, _ = key_ref.shape
    cached_len = places * pair_count // requests
    side = requests // pair_count
    request = lax.broadcasted_iota(jnp.int32, (requests, places), 0)
    place = lax.broadcasted_iota(jnp.int32, (requests, places), 1)
    place = place - lax.rem(request, jnp.int32(side)) * cached_len
    allowed = (place >= 0) & (place < column_of(lengths_in[...]))
    allowed = allowed.astype(jnp.float32)
    for h in range(group_size):
        score_ref[0, pl.ds(h, requests, stride=group_size), :] = allowed
    valid = score_ref[0] > 0.0
    copies[4].wait()
    block = side * group_size
    for j in range(cached_count):
        lanes = slice(j * HEAD_SIZE, (j + 1) * HEAD_SIZE)
        for p in range(pair_count):
            here = slice(p * block, (p + 1) * block)
            turned = key_ref[p, :, lanes].T
            turned_ref[j, p] = turned
            score_ref[j, here, :] = jnp.dot(
                heads_ref[j, here, :].astype(jnp.bfloat16), turned, preferred_element_type=jnp.float32
            )
        score_ref[j] = jnp.where(valid, score_ref[j] * FACTOR, MASKED)
    for copy in copies[5:]:
        copy.wait()


def prepare(base_query, lengths, new_key, new_value, adapter_down, adapter_up, key_cache, value_cache):
    requests, features = base_query.shape
    cached_count = new_key.shape[1] // HEAD_SIZE
    rows = requests * features // (HEAD_SIZE * cached_count)
    places = key_cache.shape[1]
    held = [adapter_down, adapter_up, value_cache]
    moved = [base_query, lengths.reshape(1, requests), new_key, new_value]
    return pl.pallas_call(
        prepare_kernel,
        out_shape=[
            pltpu.VMEM((cached_count, rows, HEAD_SIZE), jnp.float32),
            pltpu.VMEM((cached_count, rows, places), jnp.float32),
            pltpu.VMEM((cached_count, rows, HEAD_SIZE), jnp.float32),
            pltpu.VMEM((cached_count, rows, HEAD_SIZE), jnp.float32),
            pltpu.VMEM((cached_count, key_cache.shape[0], HEAD_SIZE, places), key_cache.dtype),
        ]
        + [pltpu.VMEM(array.shape, array.dtype) for array in held],
        in_specs=[ANYWHERE] * 8,
        out_specs=[VMEM] * 8,
        scratch_shapes=[pltpu.VMEM(array.shape, array.dtype) for array in [*moved, key_cache]]
        + [pltpu.SemaphoreType.DMA((8,))],
        compiler_params=grant(12),
        cost_estimate=pl.CostEstimate(
            flops=0, bytes_accessed=4 * key_cache.size + 4 * adapter_up.size, transcendentals=0
        ),
        name="prepare",
    )(*[in_hbm(array) for array in [*moved, adapter_down, adapter_up, key_cache, value_cache]])


def attend_kernel(
    parts,
    heads_ref,
    score_ref,
    fresh_k_ref,
    fresh_v_ref,
    key_ref,
    value_ref,
    routing_ref,
    *refs,
):
    returned = refs[:-6]
    out_hbm, delta_ref, weight_ref, mixed_ref, out_ref, sems = refs[-6:]
    _, pair_count, _, _ = key_ref.shape
    _, rows, _ = heads_ref.shape
    requests = out_hbm.shape[0]
    group_size = rows // requests
    block = rows // pair_count
    half = lax.axis_index("tp")
    width = group_size * HEAD_SIZE
    copies = []
    cached_count = out_ref.shape[0]

    def unpack(j):
        arrived = []
        for piece in parts:
            part, at = divmod(j * len(piece), cached_count)
            at = at // len(piece) * width
            arrived.append(returned[piece[part]][half, :, at : at + width])
        arrived = jnp.concatenate(arrived, axis=0)
        delta = jnp.dot(routing_ref[...], arrived, preferred_element_type=jnp.float32)
        for h in range(group_size):
            delta_ref[j, pl.ds(h, requests, stride=group_size), :] = delta[
                :, h * HEAD_SIZE : (h + 1) * HEAD_SIZE
            ]

    def score(j):
        for p in range(pair_count):
            here = slice(p * block, (p + 1) * block)
            weight_ref[j, here, :] = jnp.dot(
                delta_ref[j, here, :].astype(jnp.bfloat16), key_ref[j, p], preferred_element_type=jnp.float32
            )

    def weigh(j):
        scores = score_ref[j] + weight_ref[j] * FACTOR
        own = (heads_ref[j] + delta_ref[j]) * fresh_k_ref[j]
        own = jnp.sum(own, axis=1, keepdims=True) * FACTOR
        highest = jnp.maximum(jnp.max(scores, axis=1, keepdims=True), own)
        weights = jnp.exp(scores - highest)
        own_weight = jnp.exp(own - highest)
        totals = jnp.sum(weights, axis=1, keepdims=True) + own_weight
        weight_ref[j] = weights
        own_b = own_weight.astype(jnp.bfloat16).astype(jnp.float32)
        delta_ref[j] = own_b * fresh_v_ref[j]
        return totals

    def mix(j, totals):
        lanes = slice(j * HEAD_SIZE, (j + 1) * HEAD_SIZE)
        for p in range(pair_count):
            here = slice(p * block, (p + 1) * block)
            mixed_ref[j, here, :] = jnp.dot(
                weight_ref[j, here, :].astype(jnp.bfloat16),
                value_ref[p, :, lanes],
                preferred_element_type=jnp.float32,
            )
        mixed_ref[j] = (mixed_ref[j] + delta_ref[j]) / totals
        for h in range(group_size):
            out_ref[j, :, h * HEAD_SIZE : (h + 1) * HEAD_SIZE] = mixed_ref[
                j, pl.ds(h, requests, stride=group_size), :
            ].astype(jnp.bfloat16)
        copy = pltpu.make_async_copy(
            out_ref.at[j], out_hbm.at[:, pl.ds(j * width, width)], sems.at[j]
        )
        copy.start()
        copies.append(copy)

    for j in range(cached_count):
        unpack(j)
    for j in range(cached_count):
        score(j)
    totals = [weigh(j) for j in range(cached_count)]
    for j in range(cached_count):
        mix(j, totals[j])
    for copy in copies:
        copy.wait()


def attend(held, routing_b, pieces):
    cached_count, rows, _ = held[0].shape
    requests = routing_b.shape[0]
    width = rows // requests * HEAD_SIZE
    parts, returned = [], []
    for piece in pieces:
        parts.append(list(range(len(returned), len(returned) + len(piece))))
        returned.extend(piece)
    return pl.pallas_call(
        functools.partial(attend_kernel, parts),
        out_shape=jax.ShapeDtypeStruct((requests, cached_count * width), jnp.bfloat16),
        in_specs=[VMEM] * (len(held) + 1 + len(returned)),
        out_specs=ANYWHERE,
        scratch_shapes=[
            pltpu.VMEM((cached_count, rows, HEAD_SIZE), jnp.float32),
            pltpu.VMEM((cached_count, rows, held[1].shape[2]), jnp.float32),
            pltpu.VMEM((cached_count, rows, HEAD_SIZE), jnp.float32),
            pltpu.VMEM((cached_count, requests, width), jnp.bfloat16),
            pltpu.SemaphoreType.DMA((cached_count,)),
        ],
        compiler_params=grant(8),
        name="attend",
    )(*held, routing_b, *returned)


def after(arrays, *tokens):
    return lax.optimization_barrier((tuple(arrays), tokens))[0]


def shards(
    hidden,
    base_query,
    key_cache,
    value_cache,
    new_key,
    new_value,
    lengths,
    request_adapter,
    adapter_store_row,
    adapter_down,
    adapter_up,
):
    request_rows = hidden.shape[0]
    pool_count = lax.axis_size("pool")
    tp_count = lax.axis_size("tp")
    capacity = max(2, 2 * request_rows // pool_count)
    owned_count = adapter_down.shape[0]
    step_count = pool_count // tp_count
    per_group = max(1, ROWS // capacity)
    group_count = step_count // per_group
    adapter_down = jnp.swapaxes(adapter_down, 1, 2)

    def move(g, rows):
        parts = []
        for k in range(per_group):
            step = g * per_group + k
            part = rows
            if per_group > 1:
                part = lax.slice_in_dim(rows, k * capacity, (k + 1) * capacity, axis=rows.ndim - 2)
            pairs = [
                (i * tp_count + c, (i ^ (tp_count * step + c)) * tp_count + c)
                for i in range(pool_count)
                for c in range(tp_count)
            ]
            parts.append(lax.ppermute(part, ("pool", "tp"), pairs))
        return parts[0] if per_group == 1 else jnp.concatenate(parts, axis=rows.ndim - 2)

    def swap(array):
        return lax.ppermute(array, "tp", [(0, 1), (1, 0)])

    far_rows, routing_b, place, spread = pack(
        hidden, request_adapter, adapter_store_row, pool_count, tp_count, capacity, owned_count, per_group * capacity
    )
    factors = [adapter_down, swap(adapter_down), adapter_up, swap(adapter_up)]
    cached_len, features = key_cache.shape[1:]
    pairs = (request_rows // 2, 2 * cached_len, features)
    *held, factors[0], factors[2], value_cache = prepare(
        *after(
            [
                base_query,
                lengths,
                new_key,
                new_value,
                adapter_down,
                adapter_up,
                key_cache.reshape(pairs),
                value_cache.reshape(pairs),
            ],
            routing_b,
        )
    )
    held = [*held, value_cache]
    *far, last = list(range(group_count // 2, group_count))
    near = list(range(group_count // 2))
    ready = after([place, spread], factors[1], factors[3])
    groups = [*pack_near(*ready, far_rows), *far_rows]
    arrived = {g: move(g, groups[g]) for g in [*far, last, *near]}
    early = serve([arrived[g] for g in far], factors)
    served = serve(after([arrived[g] for g in near], early[0]), factors)
    returned = {g: move(g, rows) for g, rows in zip(near, served)}
    returned |= {g: move(g, rows) for g, rows in zip(far, after(early, served[0]))}
    final = serve(after([arrived[last]], served[0]), factors, parts=2)
    final = [move(last, rows) for rows in final]
    whole = [returned[g] for g in range(last)]
    others = [swap(rows) for rows in whole]
    mine = [[rows] for rows in whole] + [final]
    theirs = [[rows] for rows in others] + [[swap(rows) for rows in final]]
    return attend(held, routing_b, mine + theirs)


def solution(mesh):
    placed = (
        P(("rep", "pool"), None),
        P(("rep", "pool"), "tp"),
        P(("rep", "pool"), None, "tp"),
        P(("rep", "pool"), None, "tp"),
        P(("rep", "pool"), "tp"),
        P(("rep", "pool"), "tp"),
        P(("rep", "pool")),
        P(("rep", "pool")),
        P("rep"),
        P("pool", "tp", None),
        P("pool", None, "tp"),
    )
    return jax.shard_map(
        shards, mesh=mesh, in_specs=placed, out_specs=P(("rep", "pool"), "tp"), check_vma=False
    )
```

```python
import functools
import math

import jax
import jax.numpy as jnp
from jax import lax
from jax.experimental import pallas as pl
from jax.experimental.pallas import tpu as pltpu
from jax.sharding import PartitionSpec as P

HEAD_SIZE = 128
ADAPTER_SCALE = 2.0
MASKED = -1e30
FACTOR = 1.0 / math.sqrt(HEAD_SIZE)
LANES = 128
ROWS = 16
MIB = 1024 * 1024

VMEM = pl.BlockSpec(memory_space=pltpu.VMEM)
ANYWHERE = pl.BlockSpec(memory_space=pl.ANY)


def grant(mib):
    return pltpu.CompilerParams(vmem_limit_bytes=mib * MIB)


def column_of(row):
    count = row.shape[1]
    here = lax.broadcasted_iota(jnp.int32, (count, count), 0)
    there = lax.broadcasted_iota(jnp.int32, (count, count), 1)
    spread = jnp.broadcast_to(row, (count, count))
    return jnp.sum(jnp.where(here == there, spread, 0), axis=1, keepdims=True)


def in_hbm(array):
    return pltpu.with_memory_space_constraint(array, pltpu.HBM)


def as_bf16(mask):
    return mask.astype(jnp.float32).astype(jnp.bfloat16)


def pack_kernel(pool_count, tp_count, capacity, owned_count, adapter_hbm, store_hbm, hidden_hbm, *refs):
    *outs, routing_ref, place_ref, held_ref, adapter_ref, store_ref, sems, index_sems = refs
    chunks = sems.shape[0]
    step = held_ref.shape[1] // chunks
    small = [
        pltpu.make_async_copy(adapter_hbm, adapter_ref, index_sems.at[0]),
        pltpu.make_async_copy(store_hbm, store_ref, index_sems.at[1]),
    ]
    copies = [
        pltpu.make_async_copy(
            hidden_hbm.at[:, pl.ds(c * step, step)], held_ref.at[:, pl.ds(c * step, step)], sems.at[c]
        )
        for c in range(chunks)
    ]
    for copy in small + copies:
        copy.start()
    for copy in small:
        copy.wait()
    adapters = store_ref.shape[1]
    requests = adapter_ref.shape[1]
    slot_total = pool_count // tp_count * capacity
    matches = lax.broadcasted_iota(jnp.int32, (adapters, requests), 0) == adapter_ref[...]
    position = jnp.sum(jnp.where(matches, column_of(store_ref[...]), 0), axis=0, keepdims=True)
    owner = lax.div(position, jnp.int32(owned_count))
    held = position - owner * owned_count
    distance = lax.bitwise_xor(owner, jnp.broadcast_to(lax.axis_index("pool"), owner.shape))
    step_of = lax.div(distance, jnp.int32(tp_count))
    mine = distance - step_of * tp_count == lax.axis_index("tp")
    earlier = lax.broadcasted_iota(jnp.int32, (requests, requests), 0) < lax.broadcasted_iota(
        jnp.int32, (requests, requests), 1
    )
    same = column_of(owner) == owner
    rank = jnp.sum(jnp.where(same & earlier, 1, 0), axis=0, keepdims=True)
    target = step_of * capacity + rank + jnp.where(mine, 0, slot_total)
    place_ref[0:1, :] = target
    place_ref[1:2, :] = held
    for copy in copies:
        copy.wait()
    pack_rows(target, held, held_ref, slot_total // 2, outs)
    back = lax.broadcasted_iota(jnp.int32, (requests, tp_count * slot_total), 1) == column_of(target)
    routing_ref[...] = as_bf16(back)


def pack_rows(target, held, held_ref, first, outs):
    width = held_ref.shape[1]
    requests = held_ref.shape[0]
    count = sum(out.shape[0] for out in outs)
    routing = lax.broadcasted_iota(jnp.int32, (count, requests), 0) + first == target
    held_slot = jnp.sum(jnp.where(routing, held, 0), axis=1, keepdims=True)
    tags = jnp.broadcast_to(held_slot, (count, LANES)).astype(jnp.float32).astype(jnp.bfloat16)
    routing_b = as_bf16(routing)
    chunks = 4
    step = width // chunks
    for c in range(chunks):
        columns = slice(c * step, (c + 1) * step)
        packed = jnp.dot(
            routing_b, held_ref[:, columns], preferred_element_type=jnp.float32
        ).astype(jnp.bfloat16)
        for g, out in enumerate(outs):
            out[:, columns] = packed[g * out.shape[0] : (g + 1) * out.shape[0]]
    for g, out in enumerate(outs):
        out[:, width:] = tags[g * out.shape[0] : (g + 1) * out.shape[0]]


def pack_near_kernel(place_ref, held_ref, *outs):
    pack_rows(place_ref[0:1, :], place_ref[1:2, :], held_ref, 0, outs)


def pack(hidden, request_adapter, adapter_store_row, pool_count, tp_count, capacity, owned_count, group_rows):
    requests, width = hidden.shape
    adapters = adapter_store_row.shape[0]
    slot_total = pool_count // tp_count * capacity
    group_count = slot_total // group_rows // 2
    chunks = 4
    rows = [pltpu.VMEM((group_rows, width + LANES), jnp.bfloat16)] * group_count
    *far, routing_b, place, held = pl.pallas_call(
        functools.partial(pack_kernel, pool_count, tp_count, capacity, owned_count),
        out_shape=rows
        + [
            pltpu.VMEM((requests, tp_count * slot_total), jnp.bfloat16),
            pltpu.VMEM((2, requests), jnp.int32),
            pltpu.VMEM((requests, width), jnp.bfloat16),
        ],
        in_specs=[ANYWHERE] * 3,
        out_specs=[VMEM] * (group_count + 3),
        scratch_shapes=[
            pltpu.VMEM((1, requests), jnp.int32),
            pltpu.VMEM((1, adapters), jnp.int32),
            pltpu.SemaphoreType.DMA((chunks,)),
            pltpu.SemaphoreType.DMA((2,)),
        ],
        compiler_params=grant(8),
        name="pack",
    )(
        in_hbm(request_adapter.reshape(1, requests)),
        in_hbm(adapter_store_row.reshape(1, adapters)),
        in_hbm(hidden),
    )
    return far, routing_b, place, held


def pack_near(place, held, like):
    return pl.pallas_call(
        pack_near_kernel,
        out_shape=[pltpu.VMEM(row.shape, row.dtype) for row in like],
        in_specs=[VMEM] * 2,
        out_specs=[VMEM] * len(like),
        compiler_params=grant(8),
        name="pack_near",
    )(place, held)


def serve_kernel(count, parts, *refs):
    rows, (down_ref, down_far_ref, up_ref, up_far_ref), outs = (
        refs[:count],
        refs[count : count + 4],
        refs[count + 4 :],
    )
    owned_count, rank, width = down_ref.shape
    here = lax.axis_index("tp")
    there = 1 - here
    tags = jnp.concatenate([row[:, 2 * width : 2 * width + 1] for row in rows], axis=0)
    tags = tags.astype(jnp.float32)
    middle = jnp.zeros((tags.shape[0], rank), jnp.float32)
    for half, factors in ((here, down_ref), (there, down_far_ref)):
        columns = pl.ds(pl.multiple_of(half * width, LANES), width)
        features = jnp.concatenate([row[:, columns] for row in rows], axis=0)
        for slot in range(owned_count):
            partial = lax.dot_general(
                features,
                factors[slot],
                (((1,), (1,)), ((), ())),
                preferred_element_type=jnp.float32,
            )
            middle = middle + jnp.where(tags == float(slot), partial, 0.0)
    for out in outs:
        if out.shape[2] > width // parts:
            out[:, :, width // parts :] = jnp.zeros((2, out.shape[1], out.shape[2] - width // parts), jnp.bfloat16)
    middle = middle.astype(jnp.bfloat16).astype(jnp.float32)
    chosen = jnp.concatenate(
        [jnp.where(tags == float(slot), middle, 0.0) for slot in range(owned_count)], axis=1
    ).astype(jnp.bfloat16)
    step = min(width, 1024)
    for half, factors in ((here, up_ref), (there, up_far_ref)):
        for c in range(width // step):
            columns = slice(c * step, (c + 1) * step)
            stacked = jnp.concatenate([factors[slot, :, columns] for slot in range(owned_count)], axis=0)
            total = jnp.dot(chosen, stacked, preferred_element_type=jnp.float32)
            total = (ADAPTER_SCALE * total).astype(jnp.bfloat16)
            at = 0
            for k in range(len(rows)):
                part, column = divmod(c * step, width // parts)
                out = outs[k * parts + part]
                out[half, :, column : column + step] = total[at : at + out.shape[1]]
                at += out.shape[1]


def serve(rows, factors, parts=1, extra=0):
    width = factors[0].shape[2]
    return pl.pallas_call(
        functools.partial(serve_kernel, len(rows), parts),
        out_shape=[
            pltpu.VMEM((2, row.shape[0], width // parts + extra * (part == parts - 1)), jnp.bfloat16)
            for row in rows
            for part in range(parts)
        ],
        in_specs=[VMEM] * (len(rows) + 4),
        out_specs=[VMEM] * (len(rows) * parts),
        compiler_params=grant(8),
        name="serve",
    )(*rows, *factors)


def prepare_kernel(
    base_hbm,
    lengths_hbm,
    fresh_k_hbm,
    fresh_v_hbm,
    down_hbm,
    up_hbm,
    key_hbm,
    value_hbm,
    heads_ref,
    score_ref,
    fresh_k_ref,
    fresh_v_ref,
    turned_ref,
    down_ref,
    up_ref,
    value_ref,
    base_in,
    lengths_in,
    fresh_k_in,
    fresh_v_in,
    key_ref,
    sems,
):
    pairs = [
        (lengths_hbm, lengths_in),
        (base_hbm, base_in),
        (fresh_k_hbm, fresh_k_in),
        (fresh_v_hbm, fresh_v_in),
        (key_hbm, key_ref),
        (down_hbm, down_ref),
        (up_hbm, up_ref),
        (value_hbm, value_ref),
    ]
    copies = [pltpu.make_async_copy(*pair, sems.at[i]) for i, pair in enumerate(pairs)]
    for copy in copies:
        copy.start()
    for copy in copies[:4]:
        copy.wait()
    requests = base_in.shape[0]
    cached_count, rows, _ = heads_ref.shape
    group_size = rows // requests
    for j in range(cached_count):
        lanes = slice(j * HEAD_SIZE, (j + 1) * HEAD_SIZE)
        for h in range(group_size):
            at = (j * group_size + h) * HEAD_SIZE
            here = pl.ds(h, requests, stride=group_size)
            heads_ref[j, here, :] = base_in[:, at : at + HEAD_SIZE].astype(jnp.float32)
            fresh_k_ref[j, here, :] = fresh_k_in[:, lanes].astype(jnp.float32)
            fresh_v_ref[j, here, :] = fresh_v_in[:, lanes].astype(jnp.float32)
    pair_count, places, _ = key_ref.shape
    cached_len = places * pair_count // requests
    side = requests // pair_count
    request = lax.broadcasted_iota(jnp.int32, (requests, places), 0)
    place = lax.broadcasted_iota(jnp.int32, (requests, places), 1)
    place = place - lax.rem(request, jnp.int32(side)) * cached_len
    allowed = (place >= 0) & (place < column_of(lengths_in[...]))
    allowed = allowed.astype(jnp.float32)
    for h in range(group_size):
        score_ref[0, pl.ds(h, requests, stride=group_size), :] = allowed
    valid = score_ref[0] > 0.0
    copies[4].wait()
    block = side * group_size
    for j in range(cached_count):
        lanes = slice(j * HEAD_SIZE, (j + 1) * HEAD_SIZE)
        for p in range(pair_count):
            here = slice(p * block, (p + 1) * block)
            turned = key_ref[p, :, lanes].T
            turned_ref[j, p] = turned
            score_ref[j, here, :] = jnp.dot(
                heads_ref[j, here, :].astype(jnp.bfloat16), turned, preferred_element_type=jnp.float32
            )
        score_ref[j] = jnp.where(valid, score_ref[j] * FACTOR, MASKED)
    for copy in copies[5:]:
        copy.wait()


def prepare(base_query, lengths, new_key, new_value, adapter_down, adapter_up, key_cache, value_cache):
    requests, features = base_query.shape
    cached_count = new_key.shape[1] // HEAD_SIZE
    rows = requests * features // (HEAD_SIZE * cached_count)
    places = key_cache.shape[1]
    held = [adapter_down, adapter_up, value_cache]
    moved = [base_query, lengths.reshape(1, requests), new_key, new_value]
    return pl.pallas_call(
        prepare_kernel,
        out_shape=[
            pltpu.VMEM((cached_count, rows, HEAD_SIZE), jnp.float32),
            pltpu.VMEM((cached_count, rows, places), jnp.float32),
            pltpu.VMEM((cached_count, rows, HEAD_SIZE), jnp.float32),
            pltpu.VMEM((cached_count, rows, HEAD_SIZE), jnp.float32),
            pltpu.VMEM((cached_count, key_cache.shape[0], HEAD_SIZE, places), key_cache.dtype),
        ]
        + [pltpu.VMEM(array.shape, array.dtype) for array in held],
        in_specs=[ANYWHERE] * 8,
        out_specs=[VMEM] * 8,
        scratch_shapes=[pltpu.VMEM(array.shape, array.dtype) for array in [*moved, key_cache]]
        + [pltpu.SemaphoreType.DMA((8,))],
        compiler_params=grant(12),
        cost_estimate=pl.CostEstimate(
            flops=0, bytes_accessed=4 * key_cache.size + 4 * adapter_up.size, transcendentals=0
        ),
        name="prepare",
    )(*[in_hbm(array) for array in [*moved, adapter_down, adapter_up, key_cache, value_cache]])


def attend_kernel(
    first,
    begins,
    heads_ref,
    score_ref,
    fresh_k_ref,
    fresh_v_ref,
    key_ref,
    value_ref,
    routing_ref,
    *refs,
):
    returned = refs[: len(begins)]
    if first == 0:
        out_ref, delta_ref, weight_ref, mixed_ref = refs[len(begins) :]
    else:
        before_ref, out_hbm, delta_ref, weight_ref, mixed_ref, out_ref, sems = refs[len(begins) :]
    _, pair_count, _, _ = key_ref.shape
    _, rows, _ = heads_ref.shape
    requests = routing_ref.shape[0]
    group_size = rows // requests
    block = rows // pair_count
    half = lax.axis_index("tp")
    width = group_size * HEAD_SIZE
    copies = []
    span = range(out_ref.shape[0])

    def send(source, j):
        copy = pltpu.make_async_copy(source, out_hbm.at[:, pl.ds(j * width, width)], sems.at[j])
        copy.start()
        copies.append(copy)

    if first:
        for j in range(first):
            send(before_ref.at[j], j)

    def unpack(j):
        arrived = []
        for piece, begin in zip(returned, begins):
            wide = slice((first + j - begin) * width, (first + j - begin + 1) * width)
            arrived.append(piece[half, :, wide] if len(piece.shape) == 3 else piece[:, wide])
        arrived = jnp.concatenate(arrived, axis=0)
        delta = jnp.dot(routing_ref[...], arrived, preferred_element_type=jnp.float32)
        for h in range(group_size):
            delta_ref[j, pl.ds(h, requests, stride=group_size), :] = delta[
                :, h * HEAD_SIZE : (h + 1) * HEAD_SIZE
            ]

    def score(j):
        for p in range(pair_count):
            here = slice(p * block, (p + 1) * block)
            weight_ref[j, here, :] = jnp.dot(
                delta_ref[j, here, :].astype(jnp.bfloat16), key_ref[first + j, p], preferred_element_type=jnp.float32
            )

    def weigh(j):
        scores = score_ref[first + j] + weight_ref[j] * FACTOR
        own = (heads_ref[first + j] + delta_ref[j]) * fresh_k_ref[first + j]
        own = jnp.sum(own, axis=1, keepdims=True) * FACTOR
        highest = jnp.maximum(jnp.max(scores, axis=1, keepdims=True), own)
        weights = jnp.exp(scores - highest)
        own_weight = jnp.exp(own - highest)
        totals = jnp.sum(weights, axis=1, keepdims=True) + own_weight
        weight_ref[j] = weights
        own_b = own_weight.astype(jnp.bfloat16).astype(jnp.float32)
        delta_ref[j] = own_b * fresh_v_ref[first + j]
        return totals

    def mix(j, totals):
        lanes = slice((first + j) * HEAD_SIZE, (first + j + 1) * HEAD_SIZE)
        for p in range(pair_count):
            here = slice(p * block, (p + 1) * block)
            mixed_ref[j, here, :] = jnp.dot(
                weight_ref[j, here, :].astype(jnp.bfloat16),
                value_ref[p, :, lanes],
                preferred_element_type=jnp.float32,
            )
        mixed_ref[j] = (mixed_ref[j] + delta_ref[j]) / totals
        for h in range(group_size):
            out_ref[j, :, h * HEAD_SIZE : (h + 1) * HEAD_SIZE] = mixed_ref[
                j, pl.ds(h, requests, stride=group_size), :
            ].astype(jnp.bfloat16)
        if first:
            send(out_ref.at[j], first + j)

    for j in span:
        unpack(j)
    for j in span:
        score(j)
    totals = [weigh(j) for j in span]
    for j in span:
        mix(j, totals[j])
    for copy in copies:
        copy.wait()


def attend(held, routing_b, pieces, first, span, out):
    cached_count, rows, _ = held[0].shape
    requests = routing_b.shape[0]
    width = rows // requests * HEAD_SIZE
    operands = [*held, routing_b, *[piece for piece, _ in pieces]]
    some = (span, requests, width)
    scratch = [
        pltpu.VMEM((span, rows, HEAD_SIZE), jnp.float32),
        pltpu.VMEM((span, rows, held[1].shape[2]), jnp.float32),
        pltpu.VMEM((span, rows, HEAD_SIZE), jnp.float32),
    ]
    if first == 0:
        result, place = pltpu.VMEM(some, jnp.bfloat16), VMEM
    else:
        operands.append(out)
        result, place = jax.ShapeDtypeStruct((requests, cached_count * width), jnp.bfloat16), ANYWHERE
        scratch += [pltpu.VMEM(some, jnp.bfloat16), pltpu.SemaphoreType.DMA((cached_count,))]
    return pl.pallas_call(
        functools.partial(attend_kernel, first, [begin for _, begin in pieces]),
        out_shape=result,
        in_specs=[VMEM] * len(operands),
        out_specs=place,
        scratch_shapes=scratch,
        compiler_params=grant(8),
        cost_estimate=pl.CostEstimate(flops=0, bytes_accessed=0, transcendentals=0),
        name="attend",
    )(*operands)


def theirs_kernel(rows_ref, out_ref):
    out_ref[...] = rows_ref[1 - lax.axis_index("tp")]


def theirs_of(rows):
    return pl.pallas_call(
        theirs_kernel,
        out_shape=pltpu.VMEM(rows.shape[1:], rows.dtype),
        in_specs=[VMEM],
        out_specs=VMEM,
        compiler_params=grant(8),
        cost_estimate=pl.CostEstimate(flops=0, bytes_accessed=0, transcendentals=0),
        name="theirs",
    )(rows)


def after(arrays, *tokens):
    return lax.optimization_barrier((tuple(arrays), tokens))[0]


def shards(
    hidden,
    base_query,
    key_cache,
    value_cache,
    new_key,
    new_value,
    lengths,
    request_adapter,
    adapter_store_row,
    adapter_down,
    adapter_up,
):
    request_rows = hidden.shape[0]
    pool_count = lax.axis_size("pool")
    tp_count = lax.axis_size("tp")
    capacity = max(2, 2 * request_rows // pool_count)
    owned_count = adapter_down.shape[0]
    step_count = pool_count // tp_count
    per_group = max(1, ROWS // capacity)
    group_count = step_count // per_group
    adapter_down = jnp.swapaxes(adapter_down, 1, 2)

    def move(g, rows):
        parts = []
        for k in range(per_group):
            step = g * per_group + k
            part = rows
            if per_group > 1:
                part = lax.slice_in_dim(rows, k * capacity, (k + 1) * capacity, axis=rows.ndim - 2)
            pairs = [
                (i * tp_count + c, (i ^ (tp_count * step + c)) * tp_count + c)
                for i in range(pool_count)
                for c in range(tp_count)
            ]
            parts.append(lax.ppermute(part, ("pool", "tp"), pairs))
        return parts[0] if per_group == 1 else jnp.concatenate(parts, axis=rows.ndim - 2)

    def swap(array):
        return lax.ppermute(array, "tp", [(0, 1), (1, 0)])

    far_rows, routing_b, place, spread = pack(
        hidden, request_adapter, adapter_store_row, pool_count, tp_count, capacity, owned_count, per_group * capacity
    )
    factors = [adapter_down, swap(adapter_down), adapter_up, swap(adapter_up)]
    cached_len, features = key_cache.shape[1:]
    pairs = (request_rows // 2, 2 * cached_len, features)
    *held, factors[0], factors[2], value_cache = prepare(
        *after(
            [
                base_query,
                lengths,
                new_key,
                new_value,
                adapter_down,
                adapter_up,
                key_cache.reshape(pairs),
                value_cache.reshape(pairs),
            ],
            routing_b,
        )
    )
    held = [*held, value_cache]
    *far, last = list(range(group_count // 2, group_count))
    near = list(range(group_count // 2))
    ready = after([place, spread], factors[1], factors[3])
    groups = [*pack_near(*ready, far_rows), *far_rows]
    arrived = {g: move(g, groups[g]) for g in [*far, last, *near]}
    early = serve([arrived[g] for g in far], factors)
    served = serve(after([arrived[g] for g in near], early[0]), factors)
    returned = {g: move(g, rows) for g, rows in zip(near, served)}
    returned |= {g: move(g, rows) for g, rows in zip(far, after(early, served[0]))}
    final = serve(after([arrived[last]], served[0]), factors, parts=2, extra=0)
    final = [move(last, rows) for rows in final]

    def hand(rows):
        return swap(theirs_of(rows))

    whole = [returned[g] for g in range(last)]
    others = [hand(rows) for rows in whole]
    span = features // HEAD_SIZE // len(final)
    out = None
    for k, rows in enumerate(final):
        turn = rows
        pieces = [(piece, 0) for piece in whole] + [(rows, k * span)]
        pieces += [(piece, 0) for piece in others] + [(hand(turn), k * span)]
        out = attend(held, routing_b, pieces, k * span, span, out)
    return out


def solution(mesh):
    placed = (
        P(("rep", "pool"), None),
        P(("rep", "pool"), "tp"),
        P(("rep", "pool"), None, "tp"),
        P(("rep", "pool"), None, "tp"),
        P(("rep", "pool"), "tp"),
        P(("rep", "pool"), "tp"),
        P(("rep", "pool")),
        P(("rep", "pool")),
        P("rep"),
        P("pool", "tp", None),
        P("pool", None, "tp"),
    )
    return jax.shard_map(
        shards, mesh=mesh, in_specs=placed, out_specs=P(("rep", "pool"), "tp"), check_vma=False
    )
```

```python
import functools
import math

import jax
import jax.numpy as jnp
from jax import lax
from jax.experimental import pallas as pl
from jax.experimental.pallas import tpu as pltpu
from jax.sharding import PartitionSpec as P

HEAD_SIZE = 128
ADAPTER_SCALE = 2.0
MASKED = -1e30
FACTOR = 1.0 / math.sqrt(HEAD_SIZE)
LANES = 128
ROWS = 16
MIB = 1024 * 1024

VMEM = pl.BlockSpec(memory_space=pltpu.VMEM)
ANYWHERE = pl.BlockSpec(memory_space=pl.ANY)


def grant(mib):
    return pltpu.CompilerParams(vmem_limit_bytes=mib * MIB)


def column_of(row):
    count = row.shape[1]
    here = lax.broadcasted_iota(jnp.int32, (count, count), 0)
    there = lax.broadcasted_iota(jnp.int32, (count, count), 1)
    spread = jnp.broadcast_to(row, (count, count))
    return jnp.sum(jnp.where(here == there, spread, 0), axis=1, keepdims=True)


def in_hbm(array):
    return pltpu.with_memory_space_constraint(array, pltpu.HBM)


def as_bf16(mask):
    return mask.astype(jnp.float32).astype(jnp.bfloat16)


def pack_kernel(pool_count, tp_count, capacity, owned_count, adapter_hbm, store_hbm, hidden_hbm, *refs):
    *outs, routing_ref, place_ref, held_ref, adapter_ref, store_ref, sems, index_sems = refs
    chunks = sems.shape[0]
    step = held_ref.shape[1] // chunks
    small = [
        pltpu.make_async_copy(adapter_hbm, adapter_ref, index_sems.at[0]),
        pltpu.make_async_copy(store_hbm, store_ref, index_sems.at[1]),
    ]
    copies = [
        pltpu.make_async_copy(
            hidden_hbm.at[:, pl.ds(c * step, step)], held_ref.at[:, pl.ds(c * step, step)], sems.at[c]
        )
        for c in range(chunks)
    ]
    for copy in small + copies:
        copy.start()
    for copy in small:
        copy.wait()
    adapters = store_ref.shape[1]
    requests = adapter_ref.shape[1]
    slot_total = pool_count // tp_count * capacity
    matches = lax.broadcasted_iota(jnp.int32, (adapters, requests), 0) == adapter_ref[...]
    position = jnp.sum(jnp.where(matches, column_of(store_ref[...]), 0), axis=0, keepdims=True)
    owner = lax.div(position, jnp.int32(owned_count))
    held = position - owner * owned_count
    distance = lax.bitwise_xor(owner, jnp.broadcast_to(lax.axis_index("pool"), owner.shape))
    step_of = lax.div(distance, jnp.int32(tp_count))
    mine = distance - step_of * tp_count == lax.axis_index("tp")
    earlier = lax.broadcasted_iota(jnp.int32, (requests, requests), 0) < lax.broadcasted_iota(
        jnp.int32, (requests, requests), 1
    )
    same = column_of(owner) == owner
    rank = jnp.sum(jnp.where(same & earlier, 1, 0), axis=0, keepdims=True)
    target = step_of * capacity + rank + jnp.where(mine, 0, slot_total)
    place_ref[0:1, :] = target
    place_ref[1:2, :] = held
    for copy in copies:
        copy.wait()
    pack_rows(target, held, held_ref, slot_total // 2, outs)
    back = lax.broadcasted_iota(jnp.int32, (requests, tp_count * slot_total), 1) == column_of(target)
    routing_ref[...] = as_bf16(back)


def pack_rows(target, held, held_ref, first, outs):
    width = held_ref.shape[1]
    requests = held_ref.shape[0]
    count = sum(out.shape[0] for out in outs)
    routing = lax.broadcasted_iota(jnp.int32, (count, requests), 0) + first == target
    held_slot = jnp.sum(jnp.where(routing, held, 0), axis=1, keepdims=True)
    tags = jnp.broadcast_to(held_slot, (count, LANES)).astype(jnp.float32).astype(jnp.bfloat16)
    routing_b = as_bf16(routing)
    chunks = 4
    step = width // chunks
    for c in range(chunks):
        columns = slice(c * step, (c + 1) * step)
        packed = jnp.dot(
            routing_b, held_ref[:, columns], preferred_element_type=jnp.float32
        ).astype(jnp.bfloat16)
        for g, out in enumerate(outs):
            out[:, columns] = packed[g * out.shape[0] : (g + 1) * out.shape[0]]
    for g, out in enumerate(outs):
        out[:, width:] = tags[g * out.shape[0] : (g + 1) * out.shape[0]]


def pack_near_kernel(place_ref, held_ref, *outs):
    pack_rows(place_ref[0:1, :], place_ref[1:2, :], held_ref, 0, outs)


def pack(hidden, request_adapter, adapter_store_row, pool_count, tp_count, capacity, owned_count, group_rows):
    requests, width = hidden.shape
    adapters = adapter_store_row.shape[0]
    slot_total = pool_count // tp_count * capacity
    group_count = slot_total // group_rows // 2
    chunks = 4
    rows = [pltpu.VMEM((group_rows, width + LANES), jnp.bfloat16)] * group_count
    *far, routing_b, place, held = pl.pallas_call(
        functools.partial(pack_kernel, pool_count, tp_count, capacity, owned_count),
        out_shape=rows
        + [
            pltpu.VMEM((requests, tp_count * slot_total), jnp.bfloat16),
            pltpu.VMEM((2, requests), jnp.int32),
            pltpu.VMEM((requests, width), jnp.bfloat16),
        ],
        in_specs=[ANYWHERE] * 3,
        out_specs=[VMEM] * (group_count + 3),
        scratch_shapes=[
            pltpu.VMEM((1, requests), jnp.int32),
            pltpu.VMEM((1, adapters), jnp.int32),
            pltpu.SemaphoreType.DMA((chunks,)),
            pltpu.SemaphoreType.DMA((2,)),
        ],
        compiler_params=grant(8),
        name="pack",
    )(
        in_hbm(request_adapter.reshape(1, requests)),
        in_hbm(adapter_store_row.reshape(1, adapters)),
        in_hbm(hidden),
    )
    return far, routing_b, place, held


def pack_near(place, held, like):
    return pl.pallas_call(
        pack_near_kernel,
        out_shape=[pltpu.VMEM(row.shape, row.dtype) for row in like],
        in_specs=[VMEM] * 2,
        out_specs=[VMEM] * len(like),
        compiler_params=grant(8),
        name="pack_near",
    )(place, held)


def serve_kernel(count, parts, *refs):
    rows, (down_ref, down_far_ref, up_ref, up_far_ref), outs = (
        refs[:count],
        refs[count : count + 4],
        refs[count + 4 :],
    )
    owned_count, rank, width = down_ref.shape
    here = lax.axis_index("tp")
    there = 1 - here
    tags = jnp.concatenate([row[:, 2 * width : 2 * width + 1] for row in rows], axis=0)
    tags = tags.astype(jnp.float32)
    middle = jnp.zeros((tags.shape[0], rank), jnp.float32)
    for half, factors in ((here, down_ref), (there, down_far_ref)):
        columns = pl.ds(pl.multiple_of(half * width, LANES), width)
        features = jnp.concatenate([row[:, columns] for row in rows], axis=0)
        for slot in range(owned_count):
            partial = lax.dot_general(
                features,
                factors[slot],
                (((1,), (1,)), ((), ())),
                preferred_element_type=jnp.float32,
            )
            middle = middle + jnp.where(tags == float(slot), partial, 0.0)
    for out in outs:
        if out.shape[2] > width // parts:
            out[:, :, width // parts :] = jnp.zeros((2, out.shape[1], out.shape[2] - width // parts), jnp.bfloat16)
    middle = middle.astype(jnp.bfloat16).astype(jnp.float32)
    chosen = jnp.concatenate(
        [jnp.where(tags == float(slot), middle, 0.0) for slot in range(owned_count)], axis=1
    ).astype(jnp.bfloat16)
    step = min(width, 1024)
    for half, factors in ((here, up_ref), (there, up_far_ref)):
        for c in range(width // step):
            columns = slice(c * step, (c + 1) * step)
            stacked = jnp.concatenate([factors[slot, :, columns] for slot in range(owned_count)], axis=0)
            total = jnp.dot(chosen, stacked, preferred_element_type=jnp.float32)
            total = (ADAPTER_SCALE * total).astype(jnp.bfloat16)
            at = 0
            for k in range(len(rows)):
                part, column = divmod(c * step, width // parts)
                out = outs[k * parts + part]
                out[half, :, column : column + step] = total[at : at + out.shape[1]]
                at += out.shape[1]


def serve(rows, factors, parts=1, extra=0):
    width = factors[0].shape[2]
    return pl.pallas_call(
        functools.partial(serve_kernel, len(rows), parts),
        out_shape=[
            pltpu.VMEM((2, row.shape[0], width // parts + extra * (part == parts - 1)), jnp.bfloat16)
            for row in rows
            for part in range(parts)
        ],
        in_specs=[VMEM] * (len(rows) + 4),
        out_specs=[VMEM] * (len(rows) * parts),
        compiler_params=grant(8),
        name="serve",
    )(*rows, *factors)


def prepare_kernel(
    base_hbm,
    lengths_hbm,
    fresh_k_hbm,
    fresh_v_hbm,
    down_hbm,
    up_hbm,
    key_hbm,
    value_hbm,
    heads_ref,
    score_ref,
    fresh_k_ref,
    fresh_v_ref,
    turned_ref,
    down_ref,
    up_ref,
    value_ref,
    base_in,
    lengths_in,
    fresh_k_in,
    fresh_v_in,
    key_ref,
    sems,
):
    pairs = [
        (lengths_hbm, lengths_in),
        (base_hbm, base_in),
        (fresh_k_hbm, fresh_k_in),
        (fresh_v_hbm, fresh_v_in),
        (key_hbm, key_ref),
        (down_hbm, down_ref),
        (up_hbm, up_ref),
        (value_hbm, value_ref),
    ]
    copies = [pltpu.make_async_copy(*pair, sems.at[i]) for i, pair in enumerate(pairs)]
    for copy in copies:
        copy.start()
    for copy in copies[:4]:
        copy.wait()
    requests = base_in.shape[0]
    cached_count, rows, _ = heads_ref.shape
    group_size = rows // requests
    for j in range(cached_count):
        lanes = slice(j * HEAD_SIZE, (j + 1) * HEAD_SIZE)
        for h in range(group_size):
            at = (j * group_size + h) * HEAD_SIZE
            here = pl.ds(h, requests, stride=group_size)
            heads_ref[j, here, :] = base_in[:, at : at + HEAD_SIZE].astype(jnp.float32)
            fresh_k_ref[j, here, :] = fresh_k_in[:, lanes].astype(jnp.float32)
            fresh_v_ref[j, here, :] = fresh_v_in[:, lanes].astype(jnp.float32)
    pair_count, places, _ = key_ref.shape
    cached_len = places * pair_count // requests
    side = requests // pair_count
    request = lax.broadcasted_iota(jnp.int32, (requests, places), 0)
    place = lax.broadcasted_iota(jnp.int32, (requests, places), 1)
    place = place - lax.rem(request, jnp.int32(side)) * cached_len
    allowed = (place >= 0) & (place < column_of(lengths_in[...]))
    allowed = allowed.astype(jnp.float32)
    for h in range(group_size):
        score_ref[0, pl.ds(h, requests, stride=group_size), :] = allowed
    valid = score_ref[0] > 0.0
    copies[4].wait()
    block = side * group_size
    for j in range(cached_count):
        lanes = slice(j * HEAD_SIZE, (j + 1) * HEAD_SIZE)
        for p in range(pair_count):
            here = slice(p * block, (p + 1) * block)
            turned = key_ref[p, :, lanes].T
            turned_ref[j, p] = turned
            score_ref[j, here, :] = jnp.dot(
                heads_ref[j, here, :].astype(jnp.bfloat16), turned, preferred_element_type=jnp.float32
            )
        score_ref[j] = jnp.where(valid, score_ref[j] * FACTOR, MASKED)
    for copy in copies[5:]:
        copy.wait()


def prepare(base_query, lengths, new_key, new_value, adapter_down, adapter_up, key_cache, value_cache):
    requests, features = base_query.shape
    cached_count = new_key.shape[1] // HEAD_SIZE
    rows = requests * features // (HEAD_SIZE * cached_count)
    places = key_cache.shape[1]
    held = [adapter_down, adapter_up, value_cache]
    moved = [base_query, lengths.reshape(1, requests), new_key, new_value]
    return pl.pallas_call(
        prepare_kernel,
        out_shape=[
            pltpu.VMEM((cached_count, rows, HEAD_SIZE), jnp.float32),
            pltpu.VMEM((cached_count, rows, places), jnp.float32),
            pltpu.VMEM((cached_count, rows, HEAD_SIZE), jnp.float32),
            pltpu.VMEM((cached_count, rows, HEAD_SIZE), jnp.float32),
            pltpu.VMEM((cached_count, key_cache.shape[0], HEAD_SIZE, places), key_cache.dtype),
        ]
        + [pltpu.VMEM(array.shape, array.dtype) for array in held],
        in_specs=[ANYWHERE] * 8,
        out_specs=[VMEM] * 8,
        scratch_shapes=[pltpu.VMEM(array.shape, array.dtype) for array in [*moved, key_cache]]
        + [pltpu.SemaphoreType.DMA((8,))],
        compiler_params=grant(12),
        cost_estimate=pl.CostEstimate(
            flops=0, bytes_accessed=4 * key_cache.size + 4 * adapter_up.size, transcendentals=0
        ),
        name="prepare",
    )(*[in_hbm(array) for array in [*moved, adapter_down, adapter_up, key_cache, value_cache]])


def attend_kernel(
    first,
    begins,
    heads_ref,
    score_ref,
    fresh_k_ref,
    fresh_v_ref,
    key_ref,
    value_ref,
    routing_ref,
    *refs,
):
    returned = refs[: len(begins)]
    if first == 0:
        out_ref, delta_ref, weight_ref, mixed_ref = refs[len(begins) :]
    else:
        before_ref, out_hbm, delta_ref, weight_ref, mixed_ref, out_ref, sems = refs[len(begins) :]
    _, pair_count, _, _ = key_ref.shape
    _, rows, _ = heads_ref.shape
    requests = routing_ref.shape[0]
    group_size = rows // requests
    block = rows // pair_count
    half = lax.axis_index("tp")
    width = group_size * HEAD_SIZE
    copies = []
    span = range(out_ref.shape[0])

    def send(source, j):
        copy = pltpu.make_async_copy(source, out_hbm.at[:, pl.ds(j * width, width)], sems.at[j])
        copy.start()
        copies.append(copy)

    if first:
        for j in range(first):
            send(before_ref.at[j], j)

    def unpack(j):
        arrived = []
        for piece, begin in zip(returned, begins):
            wide = slice((first + j - begin) * width, (first + j - begin + 1) * width)
            arrived.append(piece[half, :, wide] if len(piece.shape) == 3 else piece[:, wide])
        arrived = jnp.concatenate(arrived, axis=0)
        delta = jnp.dot(routing_ref[...], arrived, preferred_element_type=jnp.float32)
        for h in range(group_size):
            delta_ref[j, pl.ds(h, requests, stride=group_size), :] = delta[
                :, h * HEAD_SIZE : (h + 1) * HEAD_SIZE
            ]

    def score(j):
        for p in range(pair_count):
            here = slice(p * block, (p + 1) * block)
            weight_ref[j, here, :] = jnp.dot(
                delta_ref[j, here, :].astype(jnp.bfloat16), key_ref[first + j, p], preferred_element_type=jnp.float32
            )

    def weigh(j):
        scores = score_ref[first + j] + weight_ref[j] * FACTOR
        own = (heads_ref[first + j] + delta_ref[j]) * fresh_k_ref[first + j]
        own = jnp.sum(own, axis=1, keepdims=True) * FACTOR
        highest = jnp.maximum(jnp.max(scores, axis=1, keepdims=True), own)
        weights = jnp.exp(scores - highest)
        own_weight = jnp.exp(own - highest)
        totals = jnp.sum(weights, axis=1, keepdims=True) + own_weight
        weight_ref[j] = weights
        own_b = own_weight.astype(jnp.bfloat16).astype(jnp.float32)
        delta_ref[j] = own_b * fresh_v_ref[first + j]
        return totals

    def mix(j, totals):
        lanes = slice((first + j) * HEAD_SIZE, (first + j + 1) * HEAD_SIZE)
        for p in range(pair_count):
            here = slice(p * block, (p + 1) * block)
            mixed_ref[j, here, :] = jnp.dot(
                weight_ref[j, here, :].astype(jnp.bfloat16),
                value_ref[p, :, lanes],
                preferred_element_type=jnp.float32,
            )
        mixed_ref[j] = (mixed_ref[j] + delta_ref[j]) / totals
        for h in range(group_size):
            out_ref[j, :, h * HEAD_SIZE : (h + 1) * HEAD_SIZE] = mixed_ref[
                j, pl.ds(h, requests, stride=group_size), :
            ].astype(jnp.bfloat16)
        if first:
            send(out_ref.at[j], first + j)

    for j in span:
        unpack(j)
    for j in span:
        score(j)
    totals = [weigh(j) for j in span]
    for j in span:
        mix(j, totals[j])
    for copy in copies:
        copy.wait()


def attend(held, routing_b, pieces, first, span, out):
    cached_count, rows, _ = held[0].shape
    requests = routing_b.shape[0]
    width = rows // requests * HEAD_SIZE
    operands = [*held, routing_b, *[piece for piece, _ in pieces]]
    some = (span, requests, width)
    scratch = [
        pltpu.VMEM((span, rows, HEAD_SIZE), jnp.float32),
        pltpu.VMEM((span, rows, held[1].shape[2]), jnp.float32),
        pltpu.VMEM((span, rows, HEAD_SIZE), jnp.float32),
    ]
    if first == 0:
        result, place = pltpu.VMEM(some, jnp.bfloat16), VMEM
    else:
        operands.append(out)
        result, place = jax.ShapeDtypeStruct((requests, cached_count * width), jnp.bfloat16), ANYWHERE
        scratch += [pltpu.VMEM(some, jnp.bfloat16), pltpu.SemaphoreType.DMA((cached_count,))]
    return pl.pallas_call(
        functools.partial(attend_kernel, first, [begin for _, begin in pieces]),
        out_shape=result,
        in_specs=[VMEM] * len(operands),
        out_specs=place,
        scratch_shapes=scratch,
        compiler_params=grant(8),
        cost_estimate=pl.CostEstimate(flops=0, bytes_accessed=0, transcendentals=0),
        name="attend",
    )(*operands)


def theirs_kernel(rows_ref, out_ref):
    out_ref[...] = rows_ref[1 - lax.axis_index("tp")]


def theirs_of(rows):
    return pl.pallas_call(
        theirs_kernel,
        out_shape=pltpu.VMEM(rows.shape[1:], rows.dtype),
        in_specs=[VMEM],
        out_specs=VMEM,
        compiler_params=grant(8),
        cost_estimate=pl.CostEstimate(flops=0, bytes_accessed=0, transcendentals=0),
        name="theirs",
    )(rows)


def after(arrays, *tokens):
    return lax.optimization_barrier((tuple(arrays), tokens))[0]


def shards(
    hidden,
    base_query,
    key_cache,
    value_cache,
    new_key,
    new_value,
    lengths,
    request_adapter,
    adapter_store_row,
    adapter_down,
    adapter_up,
):
    request_rows = hidden.shape[0]
    pool_count = lax.axis_size("pool")
    tp_count = lax.axis_size("tp")
    capacity = max(2, 2 * request_rows // pool_count)
    owned_count = adapter_down.shape[0]
    step_count = pool_count // tp_count
    per_group = max(1, ROWS // capacity)
    group_count = step_count // per_group
    adapter_down = jnp.swapaxes(adapter_down, 1, 2)

    def move(g, rows):
        parts = []
        for k in range(per_group):
            step = g * per_group + k
            part = rows
            if per_group > 1:
                part = lax.slice_in_dim(rows, k * capacity, (k + 1) * capacity, axis=rows.ndim - 2)
            pairs = [
                (i * tp_count + c, (i ^ (tp_count * step + c)) * tp_count + c)
                for i in range(pool_count)
                for c in range(tp_count)
            ]
            parts.append(lax.ppermute(part, ("pool", "tp"), pairs))
        return parts[0] if per_group == 1 else jnp.concatenate(parts, axis=rows.ndim - 2)

    def swap(array):
        return lax.ppermute(array, "tp", [(0, 1), (1, 0)])

    far_rows, routing_b, place, spread = pack(
        hidden, request_adapter, adapter_store_row, pool_count, tp_count, capacity, owned_count, per_group * capacity
    )
    factors = [adapter_down, swap(adapter_down), adapter_up, swap(adapter_up)]
    cached_len, features = key_cache.shape[1:]
    pairs = (request_rows // 2, 2 * cached_len, features)
    *held, factors[0], factors[2], value_cache = prepare(
        *after(
            [
                base_query,
                lengths,
                new_key,
                new_value,
                adapter_down,
                adapter_up,
                key_cache.reshape(pairs),
                value_cache.reshape(pairs),
            ],
            routing_b,
        )
    )
    held = [*held, value_cache]
    *far, last = list(range(group_count // 2, group_count))
    near = list(range(group_count // 2))
    ready = after([place, spread], factors[1], factors[3])
    groups = [*pack_near(*ready, far_rows), *far_rows]
    arrived = {g: move(g, groups[g]) for g in [*far, last, *near]}
    early = serve([arrived[g] for g in far], factors)
    served = serve([arrived[g] for g in near], factors)
    returned = {g: move(g, rows) for g, rows in zip(near, served)}
    returned |= {g: move(g, rows) for g, rows in zip(far, early)}
    final = serve(after([arrived[last]], served[0]), factors, parts=2, extra=0)
    final = [move(last, rows) for rows in final]

    def hand(rows):
        return swap(theirs_of(rows))

    whole = [returned[g] for g in range(last)]
    others = [hand(rows) for rows in whole]
    span = features // HEAD_SIZE // len(final)
    out = None
    for k, rows in enumerate(final):
        turn = rows
        pieces = [(piece, 0) for piece in whole] + [(rows, k * span)]
        pieces += [(piece, 0) for piece in others] + [(hand(turn), k * span)]
        out = attend(held, routing_b, pieces, k * span, span, out)
    return out


def solution(mesh):
    placed = (
        P(("rep", "pool"), None),
        P(("rep", "pool"), "tp"),
        P(("rep", "pool"), None, "tp"),
        P(("rep", "pool"), None, "tp"),
        P(("rep", "pool"), "tp"),
        P(("rep", "pool"), "tp"),
        P(("rep", "pool")),
        P(("rep", "pool")),
        P("rep"),
        P("pool", "tp", None),
        P("pool", None, "tp"),
    )
    return jax.shard_map(
        shards, mesh=mesh, in_specs=placed, out_specs=P(("rep", "pool"), "tp"), check_vma=False
    )
```
